128 devices in a mesh: erow: 8 (over z, core), ecol: 16 (over x, y).
Axes of the slice: x: 4, y: 4, z: 4, core: 2. Of those that a mesh axis runs over, the one named last changes fastest.
Arguments:
- hidden_in: bfloat16 [512, 4, 2304], P(('erow', 'ecol')), may hold values from -6 to 6
- kda_state: float32 [512, 16, 128, 128], P('erow', 'ecol'), may hold values from -0.6 to 0.6
- query_weight: bfloat16 [2304, 2048], P(None, 'ecol'), may hold values from -0.125 to 0.125
- key_weight: bfloat16 [2304, 2048], P(None, 'ecol'), may hold values from -0.125 to 0.125
- value_weight: bfloat16 [2304, 2048], P(None, 'ecol'), may hold values from -0.125 to 0.125
- beta_weight: bfloat16 [2304, 16], P(None, 'ecol'), may hold values from -0.125 to 0.125
- decay_down: bfloat16 [2304, 128], replicated, may hold values from -0.125 to 0.125
- decay_up: bfloat16 [128, 2048], P(None, 'ecol'), may hold values from -0.5 to 0.5
- decay_log: float32 [16], P('ecol'), may hold values from -2.5 to 1
- decay_bias: float32 [2048], P('ecol'), may hold values from -4 to 4
- gate_down: bfloat16 [2304, 128], replicated, may hold values from -0.125 to 0.125
- gate_lift: bfloat16 [128, 2048], P(None, 'ecol'), may hold values from -0.5 to 0.5
- norm_gain: float32 [128], replicated, may hold values from 0.1 to 1.9
- output_weight: bfloat16 [2048, 2304], P('ecol'), may hold values from -0.125 to 0.125
- ffn_gain: float32 [2304], replicated, may hold values from 0.1 to 1.9
- expert_ids: int32 [512, 4, 8], P(('erow', 'ecol')), may hold values from 0 to 127, as said below
- route_weight: float32 [512, 4, 8], P(('erow', 'ecol')), may hold values from 0.05 to 0.6
- expert_gate: bfloat16 [128, 2304, 1024], P(('erow', 'ecol')), may hold values from -0.125 to 0.125
- expert_up: bfloat16 [128, 2304, 1024], P(('erow', 'ecol')), may hold values from -0.125 to 0.125
- expert_down: bfloat16 [128, 1024, 2304], P(('erow', 'ecol')), may hold values from -0.1875 to 0.1875
Outputs:
- mixed: bfloat16 [512, 4, 2304], P(('erow', 'ecol'))
- new_state: float32 [512, 16, 128, 128], P('erow', 'ecol')
The draws below stay inside these ranges and needn't reach their ends.
Inputs may be any that keep to these rules, and one draw needn't show every extreme that they name: `expert_ids`: each token names 8 different experts. Among the 16 tokens of one device no expert is named more than 2 times, and one and the same expert is named exactly 2 times on every device.
All inputs are finite; a program needn't handle non-finite values.
Results may differ from the reference program's by a relative error of at most 0.02.
Values may be sent and summed in bfloat16 or wider, within the bound.
No kernel may reach another device: no remote copies, remote signals or barrier semaphores. Data moves between devices by JAX's collectives and lax.ppermute only.
A program may use at most 128 MiB of HBM per device.

```python
import math
import jax
import jax.numpy as jnp
from jax import lax

D = 2304
F = 1024
H = 16
HK = 128
LR = 128
TOPK = 8
STEPS = 4
REQ_DEV = 4
REQ = 512
EXPERTS = 128
CAP = 2


def draw_expert_ids(key, part):
    key = jax.random.fold_in(key, 11)
    block_total = REQ // REQ_DEV
    row_count = STEPS * REQ_DEV
    pick_total = row_count * TOPK
    copies = CAP
    hottest = jax.random.randint(jax.random.fold_in(key, 1), (), 0, EXPERTS)
    lowest = max(1, -((EXPERTS - pick_total) // (copies - 1)))
    highest = pick_total // copies

    def one_block(block_key):
        score_key, pair_key = jax.random.split(block_key)
        numbers = jnp.arange(EXPERTS, dtype=jnp.int32)
        scores = jax.random.randint(score_key, (EXPERTS,), 0, 1 << 20) * EXPERTS + numbers
        scores = jnp.where(numbers == hottest, -1, scores)
        ordering = jnp.argsort(scores).astype(jnp.int32)
        repeated = jax.random.randint(pair_key, (), lowest, highest + 1)
        serial = jnp.arange(pick_total, dtype=jnp.int32)
        source_pos = jnp.where(serial < copies * repeated, serial // copies, serial - (copies - 1) * repeated)
        picked = ordering[source_pos]
        layout = row_count * jnp.arange(TOPK, dtype=jnp.int32)[None, :] + jnp.arange(row_count, dtype=jnp.int32)[:, None]
        return picked[layout]
    block_keys = jax.random.split(jax.random.fold_in(key, 2), block_total)
    return jax.vmap(one_block)(block_keys).reshape(REQ, STEPS, TOPK).astype(jnp.int32)


def block_levels(own_key, shape, cuts, least, high):
    loudness = 1.0
    for axis_at, blocks in cuts:
        heights = jax.random.uniform(jax.random.fold_in(jax.random.fold_in(own_key, 6), axis_at), (blocks,), jnp.float32, least / len(cuts), high / len(cuts))
        loudness = loudness * jnp.repeat(jnp.exp(heights), shape[axis_at] // blocks).reshape((-1,) + (1,) * (len(shape) - 1 - axis_at))
    return loudness


def centred(key, dims, scale, most, pieces=(), kind=jnp.bfloat16):
    drawn = jax.random.normal(key, dims, jnp.float32) * scale
    if len(pieces) > 0:
        drawn = block_levels(key, dims, pieces, -0.22, 0.18) * drawn
    return jnp.clip(drawn, min=-most, max=most).astype(kind)


def setup_inputs(seed: int = 0) -> dict:
    streams_of = jax.random.split(jax.random.key(seed), 21)
    return {
        "hidden_in": centred(streams_of[0], (REQ, STEPS, D), 1.0, 6.0, ((0, 128),)),
        "kda_state": centred(streams_of[1], (REQ, H, HK, HK), 0.1, 0.6, ((0, 8), (1, 16)), jnp.float32),
        "query_weight": centred(streams_of[2], (D, H * HK), D ** -0.5, 0.125, ((1, 16),)),
        "key_weight": centred(streams_of[3], (D, H * HK), D ** -0.5, 0.125, ((1, 16),)),
        "value_weight": centred(streams_of[4], (D, H * HK), D ** -0.5, 0.125, ((1, 16),)),
        "beta_weight": centred(streams_of[5], (D, H), D ** -0.5, 0.125, ((1, 16),)),
        "decay_down": centred(streams_of[6], (D, LR), D ** -0.5, 0.125),
        "decay_up": centred(streams_of[7], (LR, H * HK), LR ** -0.5, 0.5, ((1, 16),)),
        "decay_log": jnp.clip(-2.5 + 3.5 * jax.random.uniform(streams_of[8], (H,), jnp.float32) ** block_levels(streams_of[8], (H,), ((0, 16),), -0.2, 0.2), -2.5, 1.0),
        "decay_bias": centred(streams_of[9], (H * HK,), 1.0, 4.0, ((0, 16),), jnp.float32),
        "gate_down": centred(streams_of[10], (D, LR), D ** -0.5, 0.125),
        "gate_lift": centred(streams_of[11], (LR, H * HK), LR ** -0.5, 0.5, ((1, 16),)),
        "norm_gain": jnp.clip(1.0 + 0.18 * jax.random.normal(streams_of[12], (HK,), jnp.float32), 0.1, 1.9),
        "output_weight": centred(streams_of[13], (H * HK, D), (H * HK) ** -0.5, 0.125, ((0, 16),)),
        "ffn_gain": jnp.clip(1.0 + 0.18 * jax.random.normal(streams_of[14], (D,), jnp.float32), 0.1, 1.9),
        "expert_ids": draw_expert_ids(jax.random.fold_in(streams_of[20], 71), 0),
        "route_weight": jnp.clip(jnp.exp(math.log(0.6) - 2.4849067 * jax.random.uniform(streams_of[16], (REQ, STEPS, TOPK), jnp.float32) ** block_levels(streams_of[16], (REQ, STEPS, TOPK), ((0, 128),), -0.2, 0.2)), 0.05, 0.6),
        "expert_gate": centred(streams_of[17], (EXPERTS, D, F), D ** -0.5, 0.125, ((0, 128),)),
        "expert_up": centred(streams_of[18], (EXPERTS, D, F), D ** -0.5, 0.125, ((0, 128),)),
        "expert_down": centred(streams_of[19], (EXPERTS, F, D), F ** -0.5, 0.1875, ((0, 128),)),
    }


EPSILON = 1e-06
HIGHEST = lax.Precision.HIGHEST

def unit_rows(vectors):
    return vectors * lax.rsqrt(lax.optimization_barrier(jnp.sum(vectors * vectors, -1, keepdims=True)) + EPSILON)

def rms_scale(vectors):
    return vectors * lax.rsqrt(lax.optimization_barrier(jnp.mean(vectors * vectors, -1, keepdims=True)) + EPSILON)

def project(tokens, query_weight, key_weight, value_weight, beta_weight, decay_down, decay_up, decay_log, decay_bias, gate_down, gate_lift, head_size):
    row_total = tokens.shape[0]
    head_count = query_weight.shape[1] // head_size
    shape = (row_total, head_count, head_size)
    queries = unit_rows(jnp.dot(tokens, query_weight, preferred_element_type=jnp.float32).reshape(shape)) * head_size ** (-0.5)
    key_rows = unit_rows(jnp.dot(tokens, key_weight, preferred_element_type=jnp.float32).reshape(shape))
    values = jnp.dot(tokens, value_weight, preferred_element_type=jnp.float32).reshape(shape)
    write_rate = jax.nn.sigmoid(jnp.dot(tokens, beta_weight, preferred_element_type=jnp.float32))
    decay_low = jnp.dot(tokens, decay_down, preferred_element_type=jnp.float32).astype(jnp.bfloat16)
    decay_pre = jnp.dot(decay_low, decay_up, preferred_element_type=jnp.float32) + decay_bias
    log_decay = -jnp.exp(jnp.repeat(decay_log, head_size)) * jax.nn.softplus(decay_pre)
    factor = jnp.exp(log_decay).reshape(shape)
    gate_low = jnp.dot(tokens, gate_down, preferred_element_type=jnp.float32).astype(jnp.bfloat16)
    out_gate = jax.nn.sigmoid(jnp.dot(gate_low, gate_lift, preferred_element_type=jnp.float32)).reshape(shape)
    return (queries, key_rows, values, factor, write_rate, out_gate)

def delta_head(memory, queries, key_rows, values, factor, write_rate):
    outputs = []
    for position in range(queries.shape[1]):
        memory = memory * factor[:, position, :, None]
        predicted = jnp.einsum('rkv,rk->rv', memory, key_rows[:, position], precision=HIGHEST)
        update = write_rate[:, position, None, None] * key_rows[:, position, :, None] * (values[:, position] - predicted)[:, None, :]
        memory = memory + update
        outputs.append(jnp.einsum('rkv,rk->rv', memory, queries[:, position], precision=HIGHEST))
    return (memory, jnp.stack(outputs, 1))

def routed_sum(normed, expert_ids, route_weight, expert_gate, expert_up, expert_down):
    block_rows = 32
    expert_total = expert_gate.shape[0]
    pick_count = expert_ids.shape[-1]
    flat_ids = expert_ids.reshape(-1).astype(jnp.int32)
    flat_weights = route_weight.reshape(-1)
    pair_total = flat_ids.shape[0]
    serial = jnp.arange(pair_total, dtype=jnp.int32)
    sorted_pos = jnp.argsort(flat_ids * pair_total + serial).astype(jnp.int32)
    loads = lax.optimization_barrier(jnp.sum((flat_ids[:, None] == jnp.arange(expert_total, dtype=jnp.int32)[None, :]).astype(jnp.int32), 0))
    starts = (jnp.cumsum(loads) - loads).astype(jnp.int32)
    padded = jnp.concatenate([sorted_pos, jnp.zeros((block_rows,), jnp.int32)])

    def per_expert(totals, expert):
        load = loads[expert]
        offset = starts[expert]
        gate_mat = expert_gate[expert]
        up_mat = expert_up[expert]
        down_mat = expert_down[expert]

        def one_block(block, running):
            source_pos = lax.dynamic_slice(padded, ((offset + block * block_rows).astype(jnp.int32),), (block_rows,))
            in_range = block * block_rows + jnp.arange(block_rows, dtype=jnp.int32) < load
            token_pos = source_pos // pick_count
            chosen = normed[token_pos]
            gate_act = jnp.dot(chosen, gate_mat, preferred_element_type=jnp.float32)
            up_act = jnp.dot(chosen, up_mat, preferred_element_type=jnp.float32)
            hidden = (jax.nn.silu(gate_act) * up_act).astype(jnp.bfloat16)
            produced = jnp.dot(hidden, down_mat, preferred_element_type=jnp.float32).astype(jnp.bfloat16)
            scale = jnp.where(in_range, flat_weights[source_pos], jnp.zeros((), flat_weights.dtype))
            return running.at[token_pos].add(scale[:, None] * produced.astype(jnp.float32))
        block_count = (load + block_rows - 1) // block_rows
        return (lax.fori_loop(jnp.zeros((), jnp.int32), block_count.astype(jnp.int32), one_block, totals), None)
    start_sum = jnp.zeros((normed.shape[0], normed.shape[1]), jnp.float32)
    totals, unused = lax.scan(per_expert, start_sum, jnp.arange(expert_total, dtype=jnp.int32))
    return totals

def reference(hidden_in, kda_state, query_weight, key_weight, value_weight, beta_weight, decay_down, decay_up, decay_log, decay_bias, gate_down, gate_lift, norm_gain, output_weight, ffn_gain, expert_ids, route_weight, expert_gate, expert_up, expert_down):
    requests, step_count, model_width = hidden_in.shape
    head_size = kda_state.shape[-1]
    tokens = hidden_in.reshape(requests * step_count, model_width)
    parts = project(tokens, query_weight, key_weight, value_weight, beta_weight, decay_down, decay_up, decay_log, decay_bias, gate_down, gate_lift, head_size)
    queries, key_rows, values, factor, write_rate, out_gate = [piece.reshape((requests, step_count) + piece.shape[1:]) for piece in parts]
    inputs = (jnp.moveaxis(kda_state, 1, 0), jnp.moveaxis(queries, 2, 0), jnp.moveaxis(key_rows, 2, 0), jnp.moveaxis(values, 2, 0), jnp.moveaxis(factor, 2, 0), jnp.moveaxis(write_rate, 2, 0))
    new_heads, head_out = lax.map(lambda members: delta_head(*members), inputs)
    new_state = jnp.moveaxis(new_heads, 0, 1)
    head_out = jnp.moveaxis(head_out, 0, 2)
    mixed_heads = (rms_scale(head_out) * norm_gain * out_gate).astype(jnp.bfloat16).reshape(requests * step_count, -1)
    attended = jnp.dot(mixed_heads, output_weight, preferred_element_type=jnp.float32)
    residual = (tokens.astype(jnp.float32) + attended).astype(jnp.bfloat16)
    normed = (rms_scale(residual.astype(jnp.float32)) * ffn_gain).astype(jnp.bfloat16)
    routed = routed_sum(normed, expert_ids, route_weight, expert_gate, expert_up, expert_down)
    mixed = (residual.astype(jnp.float32) + routed).astype(jnp.bfloat16).reshape(requests, step_count, model_width)
    return (mixed, new_state)
```

```python
import functools

import jax
import jax.numpy as jnp
from jax import lax
from jax.experimental import pallas as pl
from jax.experimental.pallas import tpu as pltpu
from jax.sharding import PartitionSpec as P

EPSILON = 1e-06
HIGHEST = lax.Precision.HIGHEST
F32 = jnp.float32
BF16 = jnp.bfloat16
VMEM = pl.BlockSpec(memory_space=pltpu.VMEM)


def unit_rows(vectors):
    return vectors * lax.rsqrt(jnp.sum(vectors * vectors, -1, keepdims=True) + EPSILON)


def rms_scale(vectors):
    return vectors * lax.rsqrt(jnp.mean(vectors * vectors, -1, keepdims=True) + EPSILON)


def attend_kernel(
    steps,
    tok_ref,
    wq_ref,
    wk_ref,
    wv_ref,
    wb_ref,
    dd_ref,
    gd_ref,
    du_ref,
    gl_ref,
    dl_ref,
    db_ref,
    ng_ref,
    wo_ref,
    mem_ref,
    part_ref,
    keys_ref,
    upd_ref,
    stage,
    probe,
    reply,
):
    rows, _ = tok_ref.shape
    reqs = rows // steps
    hk = wq_ref.shape[1]
    tok = tok_ref[...]

    def project(weight):
        return jnp.dot(tok, weight, preferred_element_type=F32)

    qk = project(jnp.concatenate([wq_ref[...], wk_ref[...]], axis=1))
    low = project(jnp.concatenate([dd_ref[...], gd_ref[...]], axis=1)).astype(BF16)
    vb = project(jnp.concatenate([wv_ref[...], wb_ref[...]], axis=1))
    decay_pre = jnp.dot(low[:, : dd_ref.shape[1]], du_ref[...], preferred_element_type=F32)
    decay_pre = decay_pre + db_ref[...]
    gate = jax.nn.sigmoid(
        jnp.dot(low[:, dd_ref.shape[1] :], gl_ref[...], preferred_element_type=F32)
    )
    softplus = jnp.maximum(decay_pre, 0.0) + jnp.log1p(jnp.exp(-jnp.abs(decay_pre)))
    stage[0] = unit_rows(qk[:, :hk]) * hk ** (-0.5)
    stage[1] = unit_rows(qk[:, hk:])
    stage[2] = vb[:, :hk]
    stage[3] = jax.nn.sigmoid(vb[:, hk:])
    stage[4] = jnp.exp(-jnp.exp(dl_ref[...]) * softplus)

    def at(kind, t):
        return stage[kind, pl.ds(t, reqs, stride=steps), :]

    q = [at(0, t) for t in range(steps)]
    k = [at(1, t) for t in range(steps)]
    f = [at(4, t) for t in range(steps)]
    start = []
    for t in range(steps):
        start.append(f[0] if t == 0 else start[-1] * f[t])
        probe[pl.ds(t, reqs, stride=2 * steps), :] = start[t] * k[t]
        probe[pl.ds(steps + t, reqs, stride=2 * steps), :] = start[t] * q[t]

    def one_request(r, carry):
        at_rows = pl.ds(pl.multiple_of(r * 2 * steps, 2 * steps), 2 * steps)
        reply[at_rows, :] = jnp.dot(
            probe[at_rows, :].astype(BF16), mem_ref[r].astype(BF16), preferred_element_type=F32
        )
        return carry

    lax.fori_loop(0, reqs, one_request, 0, unroll=8)

    decayed = []
    updates = []
    for t in range(steps):
        if t > 0:
            decayed = [row * f[t] for row in decayed]
        predicted = reply[pl.ds(t, reqs, stride=2 * steps), :]
        for s in range(t):
            predicted = predicted + jnp.sum(decayed[s] * k[t], -1, keepdims=True) * updates[s]
        updates.append(at(3, t) * (at(2, t) - predicted))
        decayed.append(k[t])
        head = reply[pl.ds(steps + t, reqs, stride=2 * steps), :]
        for s in range(t + 1):
            head = head + jnp.sum(decayed[s] * q[t], -1, keepdims=True) * updates[s]
        stage[0, pl.ds(t, reqs, stride=steps), :] = head
    for t in range(steps):
        keys_ref[pl.ds(t, reqs, stride=2 * steps), :] = decayed[t]
        keys_ref[pl.ds(steps + t, reqs, stride=2 * steps), :] = start[-1]
        upd_ref[pl.ds(t, reqs, stride=steps), :] = updates[t]
    mixed = (rms_scale(stage[0]) * ng_ref[...] * gate).astype(BF16)
    part_ref[...] = jnp.dot(mixed, wo_ref[...], preferred_element_type=F32).astype(BF16)


def attend(tokens, weights, memory, steps):
    rows, width = tokens.shape
    reqs, hk, _ = memory.shape
    return pl.pallas_call(
        functools.partial(attend_kernel, steps),
        out_shape=(
            jax.ShapeDtypeStruct((rows, width), BF16),
            jax.ShapeDtypeStruct((2 * rows, hk), F32),
            jax.ShapeDtypeStruct((rows, hk), F32),
        ),
        in_specs=[VMEM] * (2 + len(weights)),
        out_specs=(VMEM,) * 3,
        scratch_shapes=[
            pltpu.VMEM((5, rows, hk), F32),
            pltpu.VMEM((2 * rows, hk), F32),
            pltpu.VMEM((2 * rows, hk), F32),
        ],
        compiler_params=pltpu.CompilerParams(vmem_limit_bytes=24 * 1024 * 1024),
        cost_estimate=pl.CostEstimate(
            flops=2 * rows * width * 7 * hk + 4 * reqs * 8 * hk * hk,
            bytes_accessed=10_000_000,
            transcendentals=0,
        ),
    )(tokens, *weights, memory)


def state_kernel(steps, keys_ref, upd_ref, mem_ref, new_ref):
    count = mem_ref.shape[0]
    columns = keys_ref[...].T
    for r in range(count):
        total = mem_ref[r] * columns[:, 2 * steps * r + steps : 2 * steps * r + steps + 1]
        for s in range(steps):
            at = 2 * steps * r + s
            row = upd_ref[pl.ds(steps * r + s, 1), :]
            total = total + columns[:, at : at + 1] * row
        new_ref[r] = total


def new_memory(keys, updates, memory, steps):
    reqs, hk, _ = memory.shape
    block = 16
    return pl.pallas_call(
        functools.partial(state_kernel, steps),
        out_shape=jax.ShapeDtypeStruct(memory.shape, F32),
        grid=(reqs // block,),
        in_specs=[
            pl.BlockSpec((2 * steps * block, hk), lambda i: (i, 0)),
            pl.BlockSpec((steps * block, hk), lambda i: (i, 0)),
            pl.BlockSpec((block, hk, hk), lambda i: (i, 0, 0)),
        ],
        out_specs=pl.BlockSpec((block, hk, hk), lambda i: (i, 0, 0)),
        compiler_params=pltpu.CompilerParams(vmem_limit_bytes=16 * 1024 * 1024),
        cost_estimate=pl.CostEstimate(
            flops=9 * reqs * hk * hk, bytes_accessed=2 * reqs * hk * hk * 4, transcendentals=0
        ),
    )(keys, updates, memory)


def expert_kernel(rows_ref, gate_ref, up_ref, down_ref, out_ref, total):
    step = pl.program_id(0)
    rows = rows_ref[...]
    gate = jnp.dot(rows, gate_ref[...], preferred_element_type=F32)
    up = jnp.dot(rows, up_ref[...], preferred_element_type=F32)
    hidden = (jax.nn.silu(gate) * up).astype(BF16)
    term = jnp.dot(hidden, down_ref[...], preferred_element_type=F32)

    @pl.when(step == 0)
    def _():
        total[...] = term

    @pl.when(step > 0)
    def _():
        total[...] += term

    @pl.when(step == pl.num_programs(0) - 1)
    def _():
        out_ref[...] = total[...].astype(BF16)


def run_expert(rows, gate, up, down):
    count, width = rows.shape
    hidden = gate.shape[1]
    block = 256
    return pl.pallas_call(
        expert_kernel,
        out_shape=jax.ShapeDtypeStruct((count, width), BF16),
        grid=(hidden // block,),
        in_specs=[
            pl.BlockSpec((count, width), lambda i: (0, 0)),
            pl.BlockSpec((width, block), lambda i: (0, i)),
            pl.BlockSpec((width, block), lambda i: (0, i)),
            pl.BlockSpec((block, width), lambda i: (i, 0)),
        ],
        out_specs=pl.BlockSpec((count, width), lambda i: (0, 0)),
        scratch_shapes=[pltpu.VMEM((count, width), F32)],
        compiler_params=pltpu.CompilerParams(vmem_limit_bytes=24 * 1024 * 1024),
        cost_estimate=pl.CostEstimate(
            flops=6 * count * width * hidden,
            bytes_accessed=6 * width * hidden + 4 * count * width,
            transcendentals=count * hidden,
        ),
    )(rows, gate, up, down)


def local(
    hidden_in,
    kda_state,
    query_weight,
    key_weight,
    value_weight,
    beta_weight,
    decay_down,
    decay_up,
    decay_log,
    decay_bias,
    gate_down,
    gate_lift,
    norm_gain,
    output_weight,
    ffn_gain,
    expert_ids,
    route_weight,
    expert_gate,
    expert_up,
    expert_down,
):
    local_req, step_count, model_width = hidden_in.shape
    head_size = kda_state.shape[-1]
    grid_rows = lax.axis_size("erow")
    grid_cols = lax.axis_size("ecol")
    own_rows = local_req * step_count
    own = hidden_in.reshape(own_rows, model_width)
    gathered = lax.all_to_all(
        jnp.broadcast_to(own[None], (grid_cols, own_rows, model_width)),
        "ecol",
        split_axis=0,
        concat_axis=0,
        tiled=True,
    ).reshape(grid_cols * own_rows, model_width)
    memory = kda_state.reshape(kda_state.shape[0], head_size, head_size)
    weights = (
        query_weight,
        key_weight,
        value_weight,
        jnp.broadcast_to(beta_weight, (model_width, head_size)),
        decay_down,
        gate_down,
        decay_up,
        gate_lift,
        decay_log.reshape(1, 1),
        decay_bias.reshape(1, head_size),
        norm_gain.reshape(1, head_size),
        output_weight,
    )
    partial, keys, updates = attend(gathered, weights, memory, step_count)
    terms = lax.all_to_all(
        partial.reshape(grid_cols, own_rows, model_width),
        "ecol",
        split_axis=0,
        concat_axis=0,
        tiled=True,
    )
    new_state = new_memory(keys, updates, memory, step_count).reshape(kda_state.shape)
    attended = jnp.sum(terms.astype(F32), 0)
    residual = (own.astype(F32) + attended).astype(BF16)
    normed = (rms_scale(residual.astype(F32)) * ffn_gain).astype(BF16)
    device_count = grid_rows * grid_cols
    pick_count = expert_ids.shape[-1]
    capacity = max(2, 2 * own_rows * pick_count // device_count)
    slots_total = device_count * capacity
    flat_ids = expert_ids.reshape(-1)
    flat_weights = route_weight.reshape(-1)
    serial = jnp.arange(flat_ids.shape[0], dtype=jnp.int32)
    earlier = (flat_ids[:, None] == flat_ids[None, :]) & (serial[None, :] < serial[:, None])
    slot_of = flat_ids * capacity + jnp.sum(earlier.astype(jnp.int32), 1)
    matches = (slot_of[:, None] == jnp.arange(slots_total, dtype=jnp.int32)[None, :]).reshape(
        own_rows, pick_count, slots_total
    )
    placing = jnp.any(matches, 1).astype(BF16)
    combine = jnp.sum(jnp.where(matches, flat_weights.reshape(own_rows, pick_count, 1), 0.0), 1)
    outgoing = lax.dot_general(
        placing, normed, (((0,), (0,)), ((), ())), preferred_element_type=F32
    ).astype(BF16)
    received = lax.all_to_all(
        outgoing.reshape(device_count, capacity, model_width),
        ("erow", "ecol"),
        split_axis=0,
        concat_axis=0,
        tiled=True,
    )
    produced = run_expert(
        received.reshape(-1, model_width), expert_gate[0], expert_up[0], expert_down[0]
    )
    returned = lax.all_to_all(
        produced.reshape(received.shape), ("erow", "ecol"), split_axis=0, concat_axis=0, tiled=True
    )
    returned = returned.reshape(slots_total, model_width)
    routed = jnp.dot(combine, returned.astype(F32), precision=HIGHEST)
    mixed = (
        (residual.astype(F32) + routed).astype(BF16).reshape(local_req, step_count, model_width)
    )
    return (mixed, new_state)


def solution(mesh):
    return jax.shard_map(
        local,
        mesh=mesh,
        in_specs=(
            P(("erow", "ecol"), None, None),
            P("erow", "ecol", None, None),
            P(None, "ecol"),
            P(None, "ecol"),
            P(None, "ecol"),
            P(None, "ecol"),
            P(),
            P(None, "ecol"),
            P("ecol"),
            P("ecol"),
            P(),
            P(None, "ecol"),
            P(),
            P("ecol", None),
            P(),
            P(("erow", "ecol"), None, None),
            P(("erow", "ecol"), None, None),
            P(("erow", "ecol"), None, None),
            P(("erow", "ecol"), None, None),
            P(("erow", "ecol"), None, None),
        ),
        out_specs=(P(("erow", "ecol"), None, None), P("erow", "ecol", None, None)),
        check_vma=False,
    )
```

```python
import functools

import jax
import jax.numpy as jnp
from jax import lax
from jax.experimental import pallas as pl
from jax.experimental.pallas import tpu as pltpu
from jax.sharding import PartitionSpec as P

EPSILON = 1e-06
F32 = jnp.float32
BF16 = jnp.bfloat16
VMEM = pl.BlockSpec(memory_space=pltpu.VMEM)
HBM = pl.BlockSpec(memory_space=pltpu.HBM)


def in_hbm(array):
    return pltpu.with_memory_space_constraint(array, pltpu.HBM)


def unit_rows(vectors):
    return vectors * lax.rsqrt(jnp.sum(vectors * vectors, -1, keepdims=True) + EPSILON)


def rms_scale(vectors):
    return vectors * lax.rsqrt(jnp.mean(vectors * vectors, -1, keepdims=True) + EPSILON)


def spread_kernel(in_ref, out_hbm, send):
    copies = [
        pltpu.make_async_copy(in_ref, out_hbm.at[i], send.at[i]) for i in range(out_hbm.shape[0])
    ]
    for copy in copies:
        copy.start()
    for copy in copies:
        copy.wait()


def spread(hidden, count):
    return pl.pallas_call(
        spread_kernel,
        out_shape=pltpu.HBM((count, *hidden.shape), hidden.dtype),
        in_specs=[VMEM],
        out_specs=HBM,
        scratch_shapes=[pltpu.SemaphoreType.DMA((count,))],
        compiler_params=pltpu.CompilerParams(vmem_limit_bytes=2 * 1024 * 1024),
    )(hidden)


def attend_kernel(
    steps,
    tok_ref,
    wq_ref,
    wk_ref,
    wv_ref,
    wb_ref,
    dl_ref,
    db_ref,
    ng_ref,
    dd_hbm,
    gd_hbm,
    du_hbm,
    gl_hbm,
    wo_hbm,
    mem_hbm,
    part_ref,
    keys_hbm,
    upd_hbm,
    stage,
    probe,
    reply,
    keys_ref,
    upd_ref,
    dd_ref,
    gd_ref,
    du_ref,
    gl_ref,
    wo_ref,
    mem_ref,
    sems,
):
    width, hk = wq_ref.shape
    rows = stage.shape[1]
    reqs = rows // steps
    pairs = (
        (dd_hbm, dd_ref),
        (gd_hbm, gd_ref),
        (du_hbm, du_ref),
        (gl_hbm, gl_ref),
        (mem_hbm, mem_ref),
        (wo_hbm, wo_ref),
    )
    loads = [pltpu.make_async_copy(src, dst, sems.at[i]) for i, (src, dst) in enumerate(pairs)]
    for load in loads:
        load.start()
    tok = tok_ref[...].reshape(rows, width)

    def project(weight):
        return jnp.dot(tok, weight, preferred_element_type=F32)

    qk = project(jnp.concatenate([wq_ref[...], wk_ref[...]], axis=1))
    value = project(wv_ref[...])
    beta = lax.dot_general(
        tok,
        jnp.broadcast_to(wb_ref[...], (hk, width)),
        (((1,), (1,)), ((), ())),
        preferred_element_type=F32,
    )
    for load in loads[:4]:
        load.wait()
    low = project(jnp.concatenate([dd_ref[...], gd_ref[...]], axis=1)).astype(BF16)
    decay_pre = jnp.dot(low[:, : dd_ref.shape[1]], du_ref[...], preferred_element_type=F32)
    decay_pre = decay_pre + db_ref[...]
    gate = jax.nn.sigmoid(
        jnp.dot(low[:, dd_ref.shape[1] :], gl_ref[...], preferred_element_type=F32)
    )
    softplus = jnp.maximum(decay_pre, 0.0) + jnp.log1p(jnp.exp(-jnp.abs(decay_pre)))
    stage[0] = unit_rows(qk[:, :hk]) * hk ** (-0.5)
    stage[1] = unit_rows(qk[:, hk:])
    stage[2] = value
    stage[3] = jax.nn.sigmoid(beta)
    stage[4] = jnp.exp(-jnp.exp(dl_ref[...]) * softplus)

    def at(kind, t):
        return stage[kind, pl.ds(t, reqs, stride=steps), :]

    q = [at(0, t) for t in range(steps)]
    k = [at(1, t) for t in range(steps)]
    f = [at(4, t) for t in range(steps)]
    start = []
    for t in range(steps):
        start.append(f[0] if t == 0 else start[-1] * f[t])
        probe[pl.ds(t, reqs, stride=2 * steps), :] = start[t] * k[t]
        probe[pl.ds(steps + t, reqs, stride=2 * steps), :] = start[t] * q[t]

    loads[4].wait()

    def one_request(r, carry):
        at_rows = pl.ds(pl.multiple_of(r * 2 * steps, 2 * steps), 2 * steps)
        reply[at_rows, :] = jnp.dot(
            probe[at_rows, :].astype(BF16), mem_ref[r], preferred_element_type=F32
        )
        return carry

    lax.fori_loop(0, reqs, one_request, 0, unroll=8)

    decayed = []
    updates = []
    for t in range(steps):
        if t > 0:
            decayed = [row * f[t] for row in decayed]
        predicted = reply[pl.ds(t, reqs, stride=2 * steps), :]
        for s in range(t):
            predicted = predicted + jnp.sum(decayed[s] * k[t], -1, keepdims=True) * updates[s]
        updates.append(at(3, t) * (at(2, t) - predicted))
        decayed.append(k[t])
        head = reply[pl.ds(steps + t, reqs, stride=2 * steps), :]
        for s in range(t + 1):
            head = head + jnp.sum(decayed[s] * q[t], -1, keepdims=True) * updates[s]
        stage[0, pl.ds(t, reqs, stride=steps), :] = head
    for t in range(steps):
        keys_ref[pl.ds(t, reqs, stride=2 * steps), :] = decayed[t]
        keys_ref[pl.ds(steps + t, reqs, stride=2 * steps), :] = start[-1]
        upd_ref[pl.ds(t, reqs, stride=steps), :] = updates[t]
    stores = [
        pltpu.make_async_copy(keys_ref, keys_hbm, sems.at[6]),
        pltpu.make_async_copy(upd_ref, upd_hbm, sems.at[7]),
    ]
    for store in stores:
        store.start()
    loads[5].wait()
    mixed = (rms_scale(stage[0]) * ng_ref[...] * gate).astype(BF16)
    part_ref[...] = jnp.dot(mixed, wo_ref[...], preferred_element_type=F32).astype(BF16)
    for store in stores:
        store.wait()


def attend(tokens, weights, fetched, memory, steps):
    reqs, hk, _ = memory.shape
    rows, width = reqs * steps, tokens.shape[-1]
    fetched = [in_hbm(array) for array in (*fetched, memory)]
    return pl.pallas_call(
        functools.partial(attend_kernel, steps),
        out_shape=(
            jax.ShapeDtypeStruct((rows, width), BF16),
            pltpu.HBM((2 * rows, hk), F32),
            pltpu.HBM((rows, hk), F32),
        ),
        in_specs=[VMEM] * (1 + len(weights)) + [HBM] * len(fetched),
        out_specs=(VMEM, HBM, HBM),
        scratch_shapes=[
            pltpu.VMEM((5, rows, hk), F32),
            pltpu.VMEM((2 * rows, hk), F32),
            pltpu.VMEM((2 * rows, hk), F32),
            pltpu.VMEM((2 * rows, hk), F32),
            pltpu.VMEM((rows, hk), F32),
            *[pltpu.VMEM(array.shape, array.dtype) for array in fetched],
            pltpu.SemaphoreType.DMA((len(fetched) + 2,)),
        ],
        compiler_params=pltpu.CompilerParams(vmem_limit_bytes=32 * 1024 * 1024),
        cost_estimate=pl.CostEstimate(
            flops=2 * rows * width * 7 * hk + 4 * reqs * 8 * hk * hk,
            bytes_accessed=10_000_000,
            transcendentals=0,
        ),
    )(tokens, *weights, *fetched)


def state_kernel(steps, keys_ref, upd_ref, mem_ref, new_ref):
    count = mem_ref.shape[0]
    columns = keys_ref[...].T
    for r in range(count):
        total = mem_ref[r] * columns[:, 2 * steps * r + steps : 2 * steps * r + steps + 1]
        for s in range(steps):
            at = 2 * steps * r + s
            row = upd_ref[pl.ds(steps * r + s, 1), :]
            total = total + columns[:, at : at + 1] * row
        new_ref[r] = total


def new_memory(keys, updates, memory, steps):
    reqs, hk, _ = memory.shape
    block = 16
    return pl.pallas_call(
        functools.partial(state_kernel, steps),
        out_shape=jax.ShapeDtypeStruct(memory.shape, F32),
        grid=(reqs // block,),
        in_specs=[
            pl.BlockSpec((2 * steps * block, hk), lambda i: (i, 0)),
            pl.BlockSpec((steps * block, hk), lambda i: (i, 0)),
            pl.BlockSpec((block, hk, hk), lambda i: (i, 0, 0)),
        ],
        out_specs=pl.BlockSpec((block, hk, hk), lambda i: (i, 0, 0)),
        compiler_params=pltpu.CompilerParams(vmem_limit_bytes=16 * 1024 * 1024),
        cost_estimate=pl.CostEstimate(
            flops=9 * reqs * hk * hk, bytes_accessed=2 * reqs * hk * hk * 4, transcendentals=0
        ),
    )(in_hbm(keys), in_hbm(updates), in_hbm(memory))


def join_kernel(terms_ref, own_ref, gain_ref, place_ref, residual_ref, out_ref):
    total = own_ref[...].reshape(residual_ref.shape).astype(F32)
    attended = terms_ref[0].astype(F32)
    for i in range(1, terms_ref.shape[0]):
        attended = attended + terms_ref[i].astype(F32)
    residual = (total + attended).astype(BF16)
    residual_ref[...] = residual
    normed = (rms_scale(residual.astype(F32)) * gain_ref[...]).astype(BF16)
    sent = jnp.dot(place_ref[...], normed, preferred_element_type=F32).astype(BF16)
    out_ref[...] = sent.reshape(out_ref.shape)


def join(terms, own, gain, placing, shape):
    _, rows, width = terms.shape
    return pl.pallas_call(
        join_kernel,
        out_shape=(
            jax.ShapeDtypeStruct((rows, width), BF16),
            jax.ShapeDtypeStruct(shape, BF16),
        ),
        in_specs=[VMEM] * 4,
        out_specs=(VMEM, VMEM),
        compiler_params=pltpu.CompilerParams(vmem_limit_bytes=8 * 1024 * 1024),
        cost_estimate=pl.CostEstimate(
            flops=40_000_000_000, bytes_accessed=40_000_000, transcendentals=0
        ),
    )(terms, own, gain, placing)


def expert_kernel(rows_ref, gate_ref, up_ref, down_ref, out_ref):
    rows = rows_ref[...].reshape(-1, rows_ref.shape[-1])
    gate = jnp.dot(rows, gate_ref[...], preferred_element_type=F32)
    up = jnp.dot(rows, up_ref[...], preferred_element_type=F32)
    hidden = (jax.nn.silu(gate) * up).astype(BF16)
    out = jnp.dot(hidden, down_ref[...], preferred_element_type=F32).astype(BF16)
    out_ref[...] = out.reshape(out_ref.shape)


def run_expert(rows, gate, up, down):
    width, hidden = gate.shape
    count = rows.size // width
    return pl.pallas_call(
        expert_kernel,
        out_shape=jax.ShapeDtypeStruct(rows.shape, BF16),
        in_specs=[VMEM] * 4,
        out_specs=VMEM,
        compiler_params=pltpu.CompilerParams(vmem_limit_bytes=24 * 1024 * 1024),
        cost_estimate=pl.CostEstimate(
            flops=6 * count * width * hidden,
            bytes_accessed=6 * width * hidden + 4 * count * width,
            transcendentals=count * hidden,
        ),
    )(rows, gate, up, down)


def combine_kernel(rows_ref, residual_ref, weight_ref, out_ref):
    rows = rows_ref[...].reshape(-1, rows_ref.shape[-1])
    weight = weight_ref[...]
    high = weight.astype(BF16)
    rest = weight - high.astype(F32)
    middle = rest.astype(BF16)
    low = (rest - middle.astype(F32)).astype(BF16)
    count = weight.shape[0]
    three = jnp.dot(jnp.concatenate([high, middle, low], 0), rows, preferred_element_type=F32)
    routed = three[:count] + (three[count : 2 * count] + three[2 * count :])
    mixed = (residual_ref[...].astype(F32) + routed).astype(BF16)
    out_ref[...] = mixed.reshape(out_ref.shape)


def combine_rows(rows, residual, weight, shape):
    return pl.pallas_call(
        combine_kernel,
        out_shape=jax.ShapeDtypeStruct(shape, BF16),
        in_specs=[VMEM] * 3,
        out_specs=VMEM,
        compiler_params=pltpu.CompilerParams(vmem_limit_bytes=8 * 1024 * 1024),
    )(rows, residual, weight)


def local(
    hidden_in,
    kda_state,
    query_weight,
    key_weight,
    value_weight,
    beta_weight,
    decay_down,
    decay_up,
    decay_log,
    decay_bias,
    gate_down,
    gate_lift,
    norm_gain,
    output_weight,
    ffn_gain,
    expert_ids,
    route_weight,
    expert_gate,
    expert_up,
    expert_down,
):
    local_req, step_count, model_width = hidden_in.shape
    head_size = kda_state.shape[-1]
    grid_rows = lax.axis_size("erow")
    grid_cols = lax.axis_size("ecol")
    own_rows = local_req * step_count
    gathered = lax.all_to_all(
        spread(hidden_in, grid_cols), "ecol", split_axis=0, concat_axis=0, tiled=True
    ).reshape(grid_cols * local_req, step_count, model_width)
    memory = kda_state.reshape(kda_state.shape[0], head_size, head_size)
    weights = (
        query_weight,
        key_weight,
        value_weight,
        beta_weight.reshape(1, model_width),
        decay_log.reshape(1, 1),
        decay_bias.reshape(1, head_size),
        norm_gain.reshape(1, head_size),
    )
    fetched = (decay_down, gate_down, decay_up, gate_lift, output_weight)
    partial, keys, updates = attend(
        gathered, weights, fetched, memory.astype(BF16), step_count
    )
    terms = lax.all_to_all(
        partial.reshape(grid_cols, own_rows, model_width),
        "ecol",
        split_axis=0,
        concat_axis=0,
        tiled=True,
    )
    new_state = new_memory(keys, updates, memory, step_count).reshape(kda_state.shape)
    device_count = grid_rows * grid_cols
    pick_count = expert_ids.shape[-1]
    capacity = max(2, 2 * own_rows * pick_count // device_count)
    slots_total = device_count * capacity
    flat_ids = expert_ids.reshape(-1)
    flat_weights = route_weight.reshape(-1)
    serial = jnp.arange(flat_ids.shape[0], dtype=jnp.int32)
    earlier = (flat_ids[:, None] == flat_ids[None, :]) & (serial[None, :] < serial[:, None])
    slot_of = flat_ids * capacity + jnp.sum(earlier.astype(jnp.int32), 1)
    matches = (slot_of[:, None] == jnp.arange(slots_total, dtype=jnp.int32)[None, :]).reshape(
        own_rows, pick_count, slots_total
    )
    placing = jnp.any(matches, 1).astype(BF16).T
    combine = jnp.sum(jnp.where(matches, flat_weights.reshape(own_rows, pick_count, 1), 0.0), 1)
    residual, outgoing = join(
        terms,
        hidden_in,
        ffn_gain.reshape(1, model_width),
        placing,
        (device_count, capacity, model_width),
    )
    received = lax.all_to_all(
        outgoing,
        ("erow", "ecol"),
        split_axis=0,
        concat_axis=0,
        tiled=True,
    )
    produced = run_expert(received, expert_gate[0], expert_up[0], expert_down[0])
    returned = lax.all_to_all(
        produced.reshape(received.shape), ("erow", "ecol"), split_axis=0, concat_axis=0, tiled=True
    )
    mixed = combine_rows(returned, residual, combine, hidden_in.shape)
    return (mixed, new_state)


def solution(mesh):
    return jax.shard_map(
        local,
        mesh=mesh,
        in_specs=(
            P(("erow", "ecol"), None, None),
            P("erow", "ecol", None, None),
            P(None, "ecol"),
            P(None, "ecol"),
            P(None, "ecol"),
            P(None, "ecol"),
            P(),
            P(None, "ecol"),
            P("ecol"),
            P("ecol"),
            P(),
            P(None, "ecol"),
            P(),
            P("ecol", None),
            P(),
            P(("erow", "ecol"), None, None),
            P(("erow", "ecol"), None, None),
            P(("erow", "ecol"), None, None),
            P(("erow", "ecol"), None, None),
            P(("erow", "ecol"), None, None),
        ),
        out_specs=(P(("erow", "ecol"), None, None), P("erow", "ecol", None, None)),
        check_vma=False,
    )
```

```python
import functools
import math

import jax
import jax.numpy as jnp
from jax import lax
from jax.experimental import pallas as pl
from jax.experimental.pallas import tpu as pltpu
from jax.sharding import PartitionSpec as P

EPSILON = 1e-06
F32 = jnp.float32
BF16 = jnp.bfloat16
VMEM = pl.BlockSpec(memory_space=pltpu.VMEM)
HBM = pl.BlockSpec(memory_space=pltpu.HBM)


def in_hbm(array):
    return pltpu.with_memory_space_constraint(array, pltpu.HBM)


def unit_rows(vectors):
    return vectors * lax.rsqrt(jnp.sum(vectors * vectors, -1, keepdims=True) + EPSILON)


def rms_scale(vectors):
    return vectors * lax.rsqrt(jnp.mean(vectors * vectors, -1, keepdims=True) + EPSILON)


def own_kernel(in_ref, own_ref):
    own_ref[...] = in_ref[...].reshape(own_ref.shape)


def own_rows(hidden):
    reqs, steps, width = hidden.shape
    return pl.pallas_call(
        own_kernel,
        out_shape=jax.ShapeDtypeStruct((reqs * steps, width), BF16),
        in_specs=[VMEM],
        out_specs=VMEM,
        compiler_params=pltpu.CompilerParams(vmem_limit_bytes=2 * 1024 * 1024),
    )(hidden)


def collect_kernel(own_ref, *refs):
    *blocks, out_ref = refs
    rows, width = own_ref.shape
    out_ref[pl.ds(0, rows), :] = own_ref[...]
    for i, block in enumerate(blocks):
        out_ref[pl.ds(rows * (i + 1), rows), :] = block[...].reshape(rows, width)


def collect(own, blocks):
    rows, width = own.shape
    return pl.pallas_call(
        collect_kernel,
        out_shape=jax.ShapeDtypeStruct(((1 + len(blocks)) * rows, width), BF16),
        in_specs=[VMEM] * (1 + len(blocks)),
        out_specs=VMEM,
        compiler_params=pltpu.CompilerParams(vmem_limit_bytes=4 * 1024 * 1024),
        cost_estimate=pl.CostEstimate(
            flops=40_000_000_000, bytes_accessed=40_000_000, transcendentals=0
        ),
    )(own, *blocks)


ORDER = (2, 3, 1)


def gather_rows(hidden, grid_rows, grid_cols):
    side = math.isqrt(grid_cols)

    def shifted(array, first, amount):
        pairs = []
        for row in range(grid_rows):
            for col in range(grid_cols):
                high, low = col // side, col % side
                if (row % 2 == 0) == first:
                    low = (low + amount) % side
                else:
                    high = (high + amount) % side
                pairs.append((row * grid_cols + col, row * grid_cols + high * side + low))
        return lax.ppermute(array, ("erow", "ecol"), pairs)

    near = collect(own_rows(hidden), [shifted(hidden, True, amount) for amount in ORDER])
    return [near] + [shifted(near, False, amount) for amount in ORDER]


def place_of(piece, block, side):
    row, col = lax.axis_index("erow"), lax.axis_index("ecol")
    later, earlier = (0, *ORDER)[piece], (0, *ORDER)[block]
    even = lax.rem(row, 2) == 0
    high = lax.div(col, side) + side - jnp.where(even, later, earlier)
    low = lax.rem(col, side) + side - jnp.where(even, earlier, later)
    return lax.rem(high, side) * side + lax.rem(low, side)


def attend_kernel(
    steps,
    piece0_ref,
    piece1_ref,
    piece2_ref,
    piece3_ref,
    wq_ref,
    wk_ref,
    wv_ref,
    wb_ref,
    dl_ref,
    db_ref,
    ng_ref,
    dd_ref,
    gd_ref,
    du_ref,
    gl_ref,
    wo_ref,
    mem_ref,
    part_ref,
    keys_hbm,
    upd_hbm,
    tok_ref,
    stage,
    probe,
    reply,
    keys_ref,
    upd_ref,
    sems,
):
    width, hk = wq_ref.shape
    rows = stage.shape[1]
    reqs = rows // steps
    pieces = (piece0_ref, piece1_ref, piece2_ref, piece3_ref)
    side = len(pieces)
    size = rows // side**2
    for j, piece in enumerate(pieces):
        for i in range(side):
            start = pl.multiple_of(place_of(j, i, side) * size, size)
            tok_ref[pl.ds(start, size), :] = piece[pl.ds(size * i, size), :]
    tok = tok_ref[...]

    def project(weight):
        return jnp.dot(tok, weight, preferred_element_type=F32)

    qk = project(jnp.concatenate([wq_ref[...], wk_ref[...]], axis=1))
    value = project(wv_ref[...])
    beta = lax.dot_general(
        tok,
        jnp.broadcast_to(wb_ref[...], (8, width)),
        (((1,), (1,)), ((), ())),
        preferred_element_type=F32,
    )
    low = project(jnp.concatenate([dd_ref[...], gd_ref[...]], axis=1)).astype(BF16)
    decay_pre = jnp.dot(low[:, : dd_ref.shape[1]], du_ref[...], preferred_element_type=F32)
    decay_pre = decay_pre + db_ref[...]
    gate = jax.nn.sigmoid(
        jnp.dot(low[:, dd_ref.shape[1] :], gl_ref[...], preferred_element_type=F32)
    )
    softplus = jnp.maximum(decay_pre, 0.0) + jnp.log1p(jnp.exp(-jnp.abs(decay_pre)))
    stage[0] = unit_rows(qk[:, :hk]) * hk ** (-0.5)
    stage[1] = unit_rows(qk[:, hk:])
    stage[2] = value
    stage[3] = jnp.broadcast_to(jax.nn.sigmoid(beta[:, :1]), (rows, hk))
    stage[4] = jnp.exp(-jnp.exp(dl_ref[...]) * softplus)

    def at(kind, t):
        return stage[kind, pl.ds(t, reqs, stride=steps), :]

    q = [at(0, t) for t in range(steps)]
    k = [at(1, t) for t in range(steps)]
    f = [at(4, t) for t in range(steps)]
    start = []
    for t in range(steps):
        start.append(f[0] if t == 0 else start[-1] * f[t])
        probe[pl.ds(t, reqs, stride=2 * steps), :] = start[t] * k[t]
        probe[pl.ds(steps + t, reqs, stride=2 * steps), :] = start[t] * q[t]

    def one_request(r, carry):
        at_rows = pl.ds(pl.multiple_of(r * 2 * steps, 2 * steps), 2 * steps)
        reply[at_rows, :] = jnp.dot(
            probe[at_rows, :].astype(BF16), mem_ref[r].astype(BF16), preferred_element_type=F32
        )
        return carry

    lax.fori_loop(0, reqs, one_request, 0, unroll=64)

    decayed = []
    updates = []
    for t in range(steps):
        if t > 0:
            decayed = [row * f[t] for row in decayed]
        predicted = reply[pl.ds(t, reqs, stride=2 * steps), :]
        for s in range(t):
            predicted = predicted + jnp.sum(decayed[s] * k[t], -1, keepdims=True) * updates[s]
        updates.append(at(3, t) * (at(2, t) - predicted))
        decayed.append(k[t])
        head = reply[pl.ds(steps + t, reqs, stride=2 * steps), :]
        for s in range(t + 1):
            head = head + jnp.sum(decayed[s] * q[t], -1, keepdims=True) * updates[s]
        stage[0, pl.ds(t, reqs, stride=steps), :] = head
    for t in range(steps):
        keys_ref[pl.ds(t, reqs, stride=2 * steps), :] = decayed[t]
        keys_ref[pl.ds(steps + t, reqs, stride=2 * steps), :] = start[-1]
        upd_ref[pl.ds(t, reqs, stride=steps), :] = updates[t]
    stores = [
        pltpu.make_async_copy(keys_ref, keys_hbm, sems.at[0]),
        pltpu.make_async_copy(upd_ref, upd_hbm, sems.at[1]),
    ]
    for store in stores:
        store.start()
    mixed = (rms_scale(stage[0]) * ng_ref[...] * gate).astype(BF16)
    part_ref[...] = jnp.dot(mixed, wo_ref[...], preferred_element_type=F32).astype(BF16)
    for store in stores:
        store.wait()


def attend(pieces, weights, fetched, memory, steps):
    reqs, hk, _ = memory.shape
    rows, width = reqs * steps, pieces[0].shape[-1]
    fetched = [*fetched, memory]
    return pl.pallas_call(
        functools.partial(attend_kernel, steps),
        out_shape=(
            jax.ShapeDtypeStruct((rows, width), BF16),
            pltpu.HBM((2 * rows, hk), F32),
            pltpu.HBM((rows, hk), F32),
        ),
        in_specs=[VMEM] * (len(pieces) + len(weights) + len(fetched)),
        out_specs=(VMEM, HBM, HBM),
        scratch_shapes=[
            pltpu.VMEM((rows, width), BF16),
            pltpu.VMEM((5, rows, hk), F32),
            pltpu.VMEM((2 * rows, hk), F32),
            pltpu.VMEM((2 * rows, hk), F32),
            pltpu.VMEM((2 * rows, hk), F32),
            pltpu.VMEM((rows, hk), F32),
            pltpu.SemaphoreType.DMA((2,)),
        ],
        compiler_params=pltpu.CompilerParams(vmem_limit_bytes=12 * 1024 * 1024),
        cost_estimate=pl.CostEstimate(
            flops=2 * rows * width * 7 * hk + 4 * reqs * 8 * hk * hk,
            bytes_accessed=10_000_000,
            transcendentals=0,
        ),
    )(*pieces, *weights, *fetched)


def state_kernel(steps, keys_ref, upd_ref, mem_ref, new_ref):
    count = mem_ref.shape[0]
    columns = keys_ref[...].T
    for r in range(count):
        total = mem_ref[r] * columns[:, 2 * steps * r + steps : 2 * steps * r + steps + 1]
        for s in range(steps):
            at = 2 * steps * r + s
            row = upd_ref[pl.ds(steps * r + s, 1), :]
            total = total + columns[:, at : at + 1] * row
        new_ref[r] = total


def new_memory(keys, updates, memory, steps):
    reqs, hk, _ = memory.shape
    block = 16
    return pl.pallas_call(
        functools.partial(state_kernel, steps),
        out_shape=jax.ShapeDtypeStruct(memory.shape, F32),
        grid=(reqs // block,),
        in_specs=[
            pl.BlockSpec((2 * steps * block, hk), lambda i: (i, 0)),
            pl.BlockSpec((steps * block, hk), lambda i: (i, 0)),
            pl.BlockSpec((block, hk, hk), lambda i: (i, 0, 0)),
        ],
        out_specs=pl.BlockSpec((block, hk, hk), lambda i: (i, 0, 0)),
        compiler_params=pltpu.CompilerParams(vmem_limit_bytes=16 * 1024 * 1024),
        cost_estimate=pl.CostEstimate(
            flops=9 * reqs * hk * hk, bytes_accessed=2 * reqs * hk * hk * 4, transcendentals=0
        ),
    )(in_hbm(keys), in_hbm(updates), in_hbm(memory))


def join_kernel(terms_ref, own_ref, gain_ref, place_ref, residual_ref, out_ref):
    total = own_ref[...].reshape(residual_ref.shape).astype(F32)
    attended = terms_ref[0].astype(F32)
    for i in range(1, terms_ref.shape[0]):
        attended = attended + terms_ref[i].astype(F32)
    residual = (total + attended).astype(BF16)
    residual_ref[...] = residual
    normed = (rms_scale(residual.astype(F32)) * gain_ref[...]).astype(BF16)
    sent = jnp.dot(place_ref[...], normed, preferred_element_type=F32).astype(BF16)
    out_ref[...] = sent.reshape(out_ref.shape)


def join(terms, own, gain, placing, shape):
    _, rows, width = terms.shape
    return pl.pallas_call(
        join_kernel,
        out_shape=(
            jax.ShapeDtypeStruct((rows, width), BF16),
            jax.ShapeDtypeStruct(shape, BF16),
        ),
        in_specs=[VMEM] * 4,
        out_specs=(VMEM, VMEM),
        compiler_params=pltpu.CompilerParams(vmem_limit_bytes=8 * 1024 * 1024),
        cost_estimate=pl.CostEstimate(
            flops=40_000_000_000, bytes_accessed=40_000_000, transcendentals=0
        ),
    )(terms, own, gain, placing)


def expert_kernel(rows_ref, gate_ref, up_ref, down_ref, out_ref):
    rows = rows_ref[...].reshape(-1, rows_ref.shape[-1])
    gate = jnp.dot(rows, gate_ref[...], preferred_element_type=F32)
    up = jnp.dot(rows, up_ref[...], preferred_element_type=F32)
    hidden = (jax.nn.silu(gate) * up).astype(BF16)
    out = jnp.dot(hidden, down_ref[...], preferred_element_type=F32).astype(BF16)
    out_ref[...] = out.reshape(out_ref.shape)


def run_expert(rows, gate, up, down):
    width, hidden = gate.shape
    count = rows.size // width
    return pl.pallas_call(
        expert_kernel,
        out_shape=jax.ShapeDtypeStruct(rows.shape, BF16),
        in_specs=[VMEM] * 4,
        out_specs=VMEM,
        compiler_params=pltpu.CompilerParams(vmem_limit_bytes=24 * 1024 * 1024),
        cost_estimate=pl.CostEstimate(
            flops=6 * count * width * hidden,
            bytes_accessed=6 * width * hidden + 4 * count * width,
            transcendentals=count * hidden,
        ),
    )(rows, gate, up, down)


def combine_kernel(rows_ref, residual_ref, weight_ref, out_ref):
    rows = rows_ref[...].reshape(-1, rows_ref.shape[-1])
    weight = weight_ref[...]
    high = weight.astype(BF16)
    rest = weight - high.astype(F32)
    middle = rest.astype(BF16)
    low = (rest - middle.astype(F32)).astype(BF16)
    count = weight.shape[0]
    three = jnp.dot(jnp.concatenate([high, middle, low], 0), rows, preferred_element_type=F32)
    routed = three[:count] + (three[count : 2 * count] + three[2 * count :])
    mixed = (residual_ref[...].astype(F32) + routed).astype(BF16)
    out_ref[...] = mixed.reshape(out_ref.shape)


def combine_rows(rows, residual, weight, shape):
    return pl.pallas_call(
        combine_kernel,
        out_shape=jax.ShapeDtypeStruct(shape, BF16),
        in_specs=[VMEM] * 3,
        out_specs=VMEM,
        compiler_params=pltpu.CompilerParams(vmem_limit_bytes=8 * 1024 * 1024),
    )(rows, residual, weight)


def local(
    hidden_in,
    kda_state,
    query_weight,
    key_weight,
    value_weight,
    beta_weight,
    decay_down,
    decay_up,
    decay_log,
    decay_bias,
    gate_down,
    gate_lift,
    norm_gain,
    output_weight,
    ffn_gain,
    expert_ids,
    route_weight,
    expert_gate,
    expert_up,
    expert_down,
):
    local_req, step_count, model_width = hidden_in.shape
    head_size = kda_state.shape[-1]
    grid_rows = lax.axis_size("erow")
    grid_cols = lax.axis_size("ecol")
    own_rows = local_req * step_count
    pieces = gather_rows(hidden_in, grid_rows, grid_cols)
    memory = kda_state.reshape(kda_state.shape[0], head_size, head_size)
    weights = (
        query_weight,
        key_weight,
        value_weight,
        beta_weight.reshape(1, model_width),
        decay_log.reshape(1, 1),
        decay_bias.reshape(1, head_size),
        norm_gain.reshape(1, head_size),
    )
    fetched = (decay_down, gate_down, decay_up, gate_lift, output_weight)
    partial, keys, updates = attend(
        pieces, weights, fetched, memory, step_count
    )
    terms = lax.all_to_all(
        partial.reshape(grid_cols, own_rows, model_width),
        "ecol",
        split_axis=0,
        concat_axis=0,
        tiled=True,
    )
    new_state = new_memory(keys, updates, memory, step_count).reshape(kda_state.shape)
    device_count = grid_rows * grid_cols
    pick_count = expert_ids.shape[-1]
    capacity = max(2, 2 * own_rows * pick_count // device_count)
    slots_total = device_count * capacity
    flat_ids = expert_ids.reshape(-1)
    flat_weights = route_weight.reshape(-1)
    serial = jnp.arange(flat_ids.shape[0], dtype=jnp.int32)
    earlier = (flat_ids[:, None] == flat_ids[None, :]) & (serial[None, :] < serial[:, None])
    slot_of = flat_ids * capacity + jnp.sum(earlier.astype(jnp.int32), 1)
    matches = (slot_of[:, None] == jnp.arange(slots_total, dtype=jnp.int32)[None, :]).reshape(
        own_rows, pick_count, slots_total
    )
    placing = jnp.any(matches, 1).astype(BF16).T
    combine = jnp.sum(jnp.where(matches, flat_weights.reshape(own_rows, pick_count, 1), 0.0), 1)
    residual, outgoing = join(
        terms,
        hidden_in,
        ffn_gain.reshape(1, model_width),
        placing,
        (device_count, capacity, model_width),
    )
    received = lax.all_to_all(
        outgoing,
        ("erow", "ecol"),
        split_axis=0,
        concat_axis=0,
        tiled=True,
    )
    produced = run_expert(received, expert_gate[0], expert_up[0], expert_down[0])
    returned = lax.all_to_all(
        produced.reshape(received.shape), ("erow", "ecol"), split_axis=0, concat_axis=0, tiled=True
    )
    mixed = combine_rows(returned, residual, combine, hidden_in.shape)
    return (mixed, new_state)


def solution(mesh):
    return jax.shard_map(
        local,
        mesh=mesh,
        in_specs=(
            P(("erow", "ecol"), None, None),
            P("erow", "ecol", None, None),
            P(None, "ecol"),
            P(None, "ecol"),
            P(None, "ecol"),
            P(None, "ecol"),
            P(),
            P(None, "ecol"),
            P("ecol"),
            P("ecol"),
            P(),
            P(None, "ecol"),
            P(),
            P("ecol", None),
            P(),
            P(("erow", "ecol"), None, None),
            P(("erow", "ecol"), None, None),
            P(("erow", "ecol"), None, None),
            P(("erow", "ecol"), None, None),
            P(("erow", "ecol"), None, None),
        ),
        out_specs=(P(("erow", "ecol"), None, None), P("erow", "ecol", None, None)),
        check_vma=False,
    )
```

```python
import functools
import math

import jax
import jax.numpy as jnp
from jax import lax
from jax.experimental import pallas as pl
from jax.experimental.pallas import tpu as pltpu
from jax.sharding import PartitionSpec as P

EPSILON = 1e-06
F32 = jnp.float32
BF16 = jnp.bfloat16
VMEM = pl.BlockSpec(memory_space=pltpu.VMEM)
HBM = pl.BlockSpec(memory_space=pltpu.HBM)


def in_hbm(array):
    return pltpu.with_memory_space_constraint(array, pltpu.HBM)


def unit_rows(vectors):
    return vectors * lax.rsqrt(jnp.sum(vectors * vectors, -1, keepdims=True) + EPSILON)


def rms_scale(vectors):
    return vectors * lax.rsqrt(jnp.mean(vectors * vectors, -1, keepdims=True) + EPSILON)


def own_kernel(in_ref, own_ref):
    own_ref[...] = in_ref[...].reshape(own_ref.shape)


def own_rows(hidden):
    reqs, steps, width = hidden.shape
    return pl.pallas_call(
        own_kernel,
        out_shape=jax.ShapeDtypeStruct((reqs * steps, width), BF16),
        in_specs=[VMEM],
        out_specs=VMEM,
        compiler_params=pltpu.CompilerParams(vmem_limit_bytes=2 * 1024 * 1024),
    )(hidden)


def collect_kernel(own_ref, *refs):
    *blocks, out_ref = refs
    rows, width = own_ref.shape
    out_ref[pl.ds(0, rows), :] = own_ref[...]
    for i, block in enumerate(blocks):
        out_ref[pl.ds(rows * (i + 1), rows), :] = block[...].reshape(rows, width)


def collect(own, blocks):
    rows, width = own.shape
    return pl.pallas_call(
        collect_kernel,
        out_shape=jax.ShapeDtypeStruct(((1 + len(blocks)) * rows, width), BF16),
        in_specs=[VMEM] * (1 + len(blocks)),
        out_specs=VMEM,
        compiler_params=pltpu.CompilerParams(vmem_limit_bytes=4 * 1024 * 1024),
        cost_estimate=pl.CostEstimate(
            flops=40_000_000_000, bytes_accessed=40_000_000, transcendentals=0
        ),
    )(own, *blocks)


NEAR = (2, 1, 3)
FAR = (3, 1, 2)


def shifted(array, first, amount, grid_rows, grid_cols):
    side = math.isqrt(grid_cols)
    pairs = []
    for row in range(grid_rows):
        for col in range(grid_cols):
            high, low = col // side, col % side
            if (row % 2 == 0) == first:
                low = (low + amount) % side
            else:
                high = (high + amount) % side
            pairs.append((row * grid_cols + col, row * grid_cols + high * side + low))
    return lax.ppermute(array, ("erow", "ecol"), pairs)


def place_of(piece, block, side):
    row, col = lax.axis_index("erow"), lax.axis_index("ecol")
    later, earlier = (0, *FAR)[piece], (0, *NEAR)[block]
    even = lax.rem(row, 2) == 0
    high = lax.div(col, side) + side - jnp.where(even, later, earlier)
    low = lax.rem(col, side) + side - jnp.where(even, earlier, later)
    return lax.rem(high, side) * side + lax.rem(low, side)


def attend_kernel(steps, index, side, *refs):
    (
        tok_ref,
        wq_ref,
        wk_ref,
        wv_ref,
        wb_ref,
        dl_ref,
        db_ref,
        ng_ref,
        dd_ref,
        gd_ref,
        du_ref,
        gl_ref,
        wo_ref,
        mem_ref,
    ) = refs[:14]
    (
        part_ref,
        keys_ref,
        upd_ref,
        stage,
        probe,
        reply,
    ) = refs[14:]
    width, hk = wq_ref.shape
    rows = stage.shape[1]
    reqs = rows // steps
    per_block = reqs // side
    places = [place_of(index, i, side) for i in range(side)]
    tok = tok_ref[...]

    def project(weight):
        return jnp.dot(tok, weight, preferred_element_type=F32)

    query = project(wq_ref[...])
    key = project(wk_ref[...])
    value = project(wv_ref[...])
    beta = jnp.sum(tok.astype(F32) * wb_ref[...].astype(F32), -1, keepdims=True)
    low_decay = project(dd_ref[...]).astype(BF16)
    low_gate = project(gd_ref[...]).astype(BF16)
    decay_pre = jnp.dot(low_decay, du_ref[...], preferred_element_type=F32)
    decay_pre = decay_pre + db_ref[...]
    gate = jax.nn.sigmoid(jnp.dot(low_gate, gl_ref[...], preferred_element_type=F32))
    softplus = jnp.maximum(decay_pre, 0.0) + jnp.log1p(jnp.exp(-jnp.abs(decay_pre)))
    stage[0] = unit_rows(query) * hk ** (-0.5)
    stage[1] = unit_rows(key)
    stage[2] = value
    stage[3] = jnp.broadcast_to(jax.nn.sigmoid(beta), (rows, hk))
    rate = jnp.exp(jnp.full((1, hk), dl_ref[0], F32))
    stage[4] = jnp.exp(-rate * softplus)

    def at(kind, t):
        return stage[kind, pl.ds(t, reqs, stride=steps), :]

    q = [at(0, t) for t in range(steps)]
    k = [at(1, t) for t in range(steps)]
    f = [at(4, t) for t in range(steps)]
    start = []
    for t in range(steps):
        start.append(f[0] if t == 0 else start[-1] * f[t])
        probe[pl.ds(t, reqs, stride=2 * steps), :] = start[t] * k[t]
        probe[pl.ds(steps + t, reqs, stride=2 * steps), :] = start[t] * q[t]

    for r in range(reqs):
        at_rows = pl.ds(r * 2 * steps, 2 * steps)
        memory = mem_ref[places[r // per_block] * per_block + r % per_block]
        reply[at_rows, :] = jnp.dot(
            probe[at_rows, :].astype(BF16), memory.astype(BF16), preferred_element_type=F32
        )

    decayed = []
    updates = []
    for t in range(steps):
        if t > 0:
            decayed = [row * f[t] for row in decayed]
        predicted = reply[pl.ds(t, reqs, stride=2 * steps), :]
        for s in range(t):
            predicted = predicted + jnp.sum(decayed[s] * k[t], -1, keepdims=True) * updates[s]
        updates.append(at(3, t) * (at(2, t) - predicted))
        decayed.append(k[t])
        head = reply[pl.ds(steps + t, reqs, stride=2 * steps), :]
        for s in range(t + 1):
            head = head + jnp.sum(decayed[s] * q[t], -1, keepdims=True) * updates[s]
        stage[0, pl.ds(t, reqs, stride=steps), :] = head
    for t in range(steps):
        keys_ref[pl.ds(t, reqs, stride=2 * steps), :] = decayed[t]
        keys_ref[pl.ds(steps + t, reqs, stride=2 * steps), :] = start[-1]
        upd_ref[pl.ds(t, reqs, stride=steps), :] = updates[t]
    mixed = (rms_scale(stage[0]) * ng_ref[...] * gate).astype(BF16)
    part_ref[...] = jnp.dot(mixed, wo_ref[...], preferred_element_type=F32).astype(BF16)


def attend(index, side, piece, operands, steps):
    rows, width = piece.shape
    hk = operands[-1].shape[-1]
    in_specs = [VMEM] * (1 + len(operands))
    in_specs[5] = pl.BlockSpec(memory_space=pltpu.SMEM)
    return pl.pallas_call(
        functools.partial(attend_kernel, steps, index, side),
        out_shape=(
            jax.ShapeDtypeStruct((rows, width), BF16),
            jax.ShapeDtypeStruct((2 * rows, hk), F32),
            jax.ShapeDtypeStruct((rows, hk), F32),
        ),
        in_specs=in_specs,
        out_specs=(VMEM,) * 3,
        scratch_shapes=[
            pltpu.VMEM((5, rows, hk), F32),
            pltpu.VMEM((2 * rows, hk), F32),
            pltpu.VMEM((2 * rows, hk), F32),
        ],
        compiler_params=pltpu.CompilerParams(vmem_limit_bytes=8 * 1024 * 1024),
        cost_estimate=pl.CostEstimate(
            flops=1_500_000_000, bytes_accessed=2_000_000, transcendentals=0
        ),
    )(piece, *operands)


def middle_kernel(here_ref, *refs):
    count = (len(refs) - 1) // 2
    total = here_ref[...].astype(F32)
    for ref in refs[:count]:
        total = total + ref[...].astype(F32)
    rows = refs[count].shape[0]
    refs[count][...] = total[:rows]
    for i, ref in enumerate(refs[count + 1 :]):
        ref[...] = total[rows * (i + 1) : rows * (i + 2)].astype(BF16)


def middle(here, terms):
    width = here.shape[1]
    rows = here.shape[0] // (1 + len(terms))
    return pl.pallas_call(
        middle_kernel,
        out_shape=(jax.ShapeDtypeStruct((rows, width), F32),)
        + (jax.ShapeDtypeStruct((rows, width), BF16),) * len(terms),
        in_specs=[VMEM] * (1 + len(terms)),
        out_specs=(VMEM,) * (1 + len(terms)),
        compiler_params=pltpu.CompilerParams(vmem_limit_bytes=4 * 1024 * 1024),
    )(here, *terms)


def state_kernel(steps, side, *refs):
    keys, upds = refs[:side], refs[side : 2 * side]
    mem_hbm, new_hbm, old, new, load_sem, store_sem = refs[2 * side :]
    slots, size = old.shape[:2]
    total = side**2

    def at(b):
        start = place_of(b // side, b % side, side) * size
        return pl.ds(start, size)

    def load(b):
        return pltpu.make_async_copy(mem_hbm.at[at(b)], old.at[b % slots], load_sem.at[b % slots])

    def store(b):
        return pltpu.make_async_copy(new.at[b % slots], new_hbm.at[at(b)], store_sem.at[b % slots])

    for b in range(slots - 1):
        load(b).start()
    for b in range(total):
        load(b).wait()
        if b + slots - 1 < total:
            load(b + slots - 1).start()
        if b >= slots:
            store(b - slots).wait()
        piece, block = b // side, b % side
        height = 2 * steps * size
        columns = keys[piece][pl.ds(height * block, height), :].T
        for r in range(size):
            first = 2 * steps * r
            memory = old[b % slots, r] * columns[:, first + steps : first + steps + 1]
            for s in range(steps):
                row = upds[piece][pl.ds(steps * (size * block + r) + s, 1), :]
                memory = memory + columns[:, first + s : first + s + 1] * row
            new[b % slots, r] = memory
        store(b).start()
    for b in range(total - slots, total):
        store(b).wait()


def new_memory(keys, updates, memory, steps):
    reqs, hk, _ = memory.shape
    side = len(keys)
    size, slots = reqs // side**2, 4
    return pl.pallas_call(
        functools.partial(state_kernel, steps, side),
        out_shape=pltpu.HBM(memory.shape, F32),
        in_specs=[VMEM] * (2 * side) + [HBM],
        out_specs=HBM,
        scratch_shapes=[
            pltpu.VMEM((slots, size, hk, hk), F32),
            pltpu.VMEM((slots, size, hk, hk), F32),
            pltpu.SemaphoreType.DMA((slots,)),
            pltpu.SemaphoreType.DMA((slots,)),
        ],
        compiler_params=pltpu.CompilerParams(vmem_limit_bytes=8 * 1024 * 1024),
        cost_estimate=pl.CostEstimate(
            flops=9 * reqs * hk * hk, bytes_accessed=2 * reqs * hk * hk * 4, transcendentals=0
        ),
    )(*keys, *updates, in_hbm(memory))


def route_kernel(capacity, ids_ref, weights_ref, place_ref, combine_ref):
    rows, slots = combine_ref.shape
    picks = ids_ref.shape[-1]
    ids = ids_ref[...].reshape(rows, picks)
    weights = weights_ref[...].reshape(rows, picks)
    slot = lax.broadcasted_iota(jnp.int32, (rows, slots), 1)
    named = jnp.zeros((rows, slots), F32)
    weight = jnp.zeros((rows, slots), F32)
    for j in range(picks):
        hit = ids[:, j : j + 1] == slot // capacity
        named = jnp.where(hit, 1.0, named)
        weight = jnp.where(hit, weights[:, j : j + 1], weight)
    row = lax.broadcasted_iota(jnp.int32, (rows, rows), 0)
    earlier = (lax.broadcasted_iota(jnp.int32, (rows, rows), 1) < row).astype(BF16)
    number = jnp.dot(earlier, named.astype(BF16), preferred_element_type=F32)
    mine = (named > 0.0) & (number == (slot % capacity).astype(F32))
    place_ref[...] = jnp.where(mine, 1.0, 0.0).astype(BF16)
    combine_ref[...] = jnp.where(mine, weight, 0.0)


def route(ids, weights, capacity, slots):
    rows = ids.shape[0] * ids.shape[1]
    return pl.pallas_call(
        functools.partial(route_kernel, capacity),
        out_shape=(
            jax.ShapeDtypeStruct((rows, slots), BF16),
            jax.ShapeDtypeStruct((rows, slots), F32),
        ),
        in_specs=[VMEM] * 2,
        out_specs=(VMEM,) * 2,
        compiler_params=pltpu.CompilerParams(vmem_limit_bytes=2 * 1024 * 1024),
    )(ids, weights)


def join_kernel(own_ref, gain_ref, place_ref, *refs):
    *terms, residual_ref, out_ref = refs
    attended = terms[0][...]
    for ref in terms[1:]:
        attended = attended + ref[...].astype(F32)
    residual = (own_ref[...].astype(F32) + attended).astype(BF16)
    residual_ref[...] = residual
    gain = gain_ref[...].reshape(1, -1)
    normed = (rms_scale(residual.astype(F32)) * gain).astype(BF16)
    sent = lax.dot_general(
        place_ref[...], normed, (((0,), (0,)), ((), ())), preferred_element_type=F32
    ).astype(BF16)
    out_ref[...] = sent.reshape(out_ref.shape)


def join(terms, own, gain, placing, shape):
    rows, width = own.shape
    return pl.pallas_call(
        join_kernel,
        out_shape=(
            jax.ShapeDtypeStruct((rows, width), BF16),
            jax.ShapeDtypeStruct(shape, BF16),
        ),
        in_specs=[VMEM] * (3 + len(terms)),
        out_specs=(VMEM, VMEM),
        compiler_params=pltpu.CompilerParams(vmem_limit_bytes=8 * 1024 * 1024),
        cost_estimate=pl.CostEstimate(
            flops=40_000_000_000, bytes_accessed=40_000_000, transcendentals=0
        ),
    )(own, gain, placing, *terms)


def expert_kernel(rows_ref, gate_ref, up_ref, down_ref, out_ref):
    rows = rows_ref[...].reshape(-1, rows_ref.shape[-1])
    gate = jnp.dot(rows, gate_ref[...], preferred_element_type=F32)
    up = jnp.dot(rows, up_ref[...], preferred_element_type=F32)
    hidden = (jax.nn.silu(gate) * up).astype(BF16)
    out = jnp.dot(hidden, down_ref[...], preferred_element_type=F32).astype(BF16)
    out_ref[...] = out.reshape(out_ref.shape)


def run_expert(rows, gate, up, down):
    width, hidden = gate.shape
    count = rows.size // width
    return pl.pallas_call(
        expert_kernel,
        out_shape=jax.ShapeDtypeStruct(rows.shape, BF16),
        in_specs=[VMEM] * 4,
        out_specs=VMEM,
        compiler_params=pltpu.CompilerParams(vmem_limit_bytes=24 * 1024 * 1024),
        cost_estimate=pl.CostEstimate(
            flops=6 * count * width * hidden,
            bytes_accessed=6 * width * hidden + 4 * count * width,
            transcendentals=count * hidden,
        ),
    )(rows, gate, up, down)


def combine_kernel(rows_ref, residual_ref, weight_ref, out_ref):
    rows = rows_ref[...].reshape(-1, rows_ref.shape[-1])
    weight = weight_ref[...]
    high = weight.astype(BF16)
    rest = weight - high.astype(F32)
    middle = rest.astype(BF16)
    low = (rest - middle.astype(F32)).astype(BF16)
    count = weight.shape[0]
    three = jnp.dot(jnp.concatenate([high, middle, low], 0), rows, preferred_element_type=F32)
    routed = three[:count] + (three[count : 2 * count] + three[2 * count :])
    mixed = (residual_ref[...].astype(F32) + routed).astype(BF16)
    out_ref[...] = mixed.reshape(out_ref.shape)


def combine_rows(rows, residual, weight, shape):
    return pl.pallas_call(
        combine_kernel,
        out_shape=jax.ShapeDtypeStruct(shape, BF16),
        in_specs=[VMEM] * 3,
        out_specs=VMEM,
        compiler_params=pltpu.CompilerParams(vmem_limit_bytes=8 * 1024 * 1024),
    )(rows, residual, weight)


def local(
    hidden_in,
    kda_state,
    query_weight,
    key_weight,
    value_weight,
    beta_weight,
    decay_down,
    decay_up,
    decay_log,
    decay_bias,
    gate_down,
    gate_lift,
    norm_gain,
    output_weight,
    ffn_gain,
    expert_ids,
    route_weight,
    expert_gate,
    expert_up,
    expert_down,
):
    local_req, step_count, model_width = hidden_in.shape
    head_size = kda_state.shape[-1]
    grid_rows = lax.axis_size("erow")
    grid_cols = lax.axis_size("ecol")
    side = math.isqrt(grid_cols)
    own = own_rows(hidden_in)

    def move(array, first, amount):
        return shifted(array, first, amount, grid_rows, grid_cols)

    near = collect(own, [move(hidden_in, True, amount) for amount in NEAR])
    pieces = [near] + [move(near, False, amount) for amount in FAR]
    memory = kda_state.reshape(kda_state.shape[0], head_size, head_size)
    operands = (
        query_weight,
        key_weight,
        value_weight,
        beta_weight.reshape(1, model_width),
        decay_log,
        decay_bias.reshape(1, head_size),
        norm_gain.reshape(1, head_size),
        decay_down,
        gate_down,
        decay_up,
        gate_lift,
        output_weight,
        memory,
    )
    parts, keys, updates = zip(
        *(
            attend(index, side, piece, operands, step_count)
            for index, piece in enumerate(pieces)
        )
    )
    returned = [move(part, False, -amount) for part, amount in zip(parts[1:], FAR)]
    here, *others = middle(parts[0], returned)
    terms = [here] + [move(other, True, -amount) for other, amount in zip(others, NEAR)]
    new_state = new_memory(keys, updates, memory, step_count).reshape(kda_state.shape)
    device_count = grid_rows * grid_cols
    row_total, pick_count = local_req * step_count, expert_ids.shape[-1]
    capacity = max(2, 2 * row_total * pick_count // device_count)
    slots_total = device_count * capacity
    placing, combine = route(expert_ids, route_weight, capacity, slots_total)
    residual, outgoing = join(
        terms, own, ffn_gain, placing, (device_count, capacity, model_width)
    )
    received = lax.all_to_all(
        outgoing, ("erow", "ecol"), split_axis=0, concat_axis=0, tiled=True
    )
    produced = run_expert(received, expert_gate[0], expert_up[0], expert_down[0])
    returned = lax.all_to_all(
        produced, ("erow", "ecol"), split_axis=0, concat_axis=0, tiled=True
    )
    mixed = combine_rows(returned, residual, combine, hidden_in.shape)
    return (mixed, new_state)


def solution(mesh):
    return jax.shard_map(
        local,
        mesh=mesh,
        in_specs=(
            P(("erow", "ecol"), None, None),
            P("erow", "ecol", None, None),
            P(None, "ecol"),
            P(None, "ecol"),
            P(None, "ecol"),
            P(None, "ecol"),
            P(),
            P(None, "ecol"),
            P("ecol"),
            P("ecol"),
            P(),
            P(None, "ecol"),
            P(),
            P("ecol", None),
            P(),
            P(("erow", "ecol"), None, None),
            P(("erow", "ecol"), None, None),
            P(("erow", "ecol"), None, None),
            P(("erow", "ecol"), None, None),
            P(("erow", "ecol"), None, None),
        ),
        out_specs=(P(("erow", "ecol"), None, None), P("erow", "ecol", None, None)),
        check_vma=False,
    )
```

```python
import functools
import math

import jax
import jax.numpy as jnp
from jax import lax
from jax.experimental import pallas as pl
from jax.experimental.pallas import tpu as pltpu
from jax.sharding import PartitionSpec as P

EPSILON = 1e-06
F32 = jnp.float32
BF16 = jnp.bfloat16
VMEM = pl.BlockSpec(memory_space=pltpu.VMEM)
HBM = pl.BlockSpec(memory_space=pltpu.HBM)


def in_hbm(array):
    return pltpu.with_memory_space_constraint(array, pltpu.HBM)


def unit_rows(vectors):
    return vectors * lax.rsqrt(jnp.sum(vectors * vectors, -1, keepdims=True) + EPSILON)


def rms_scale(vectors):
    return vectors * lax.rsqrt(jnp.mean(vectors * vectors, -1, keepdims=True) + EPSILON)


def own_kernel(in_ref, own_ref):
    own_ref[...] = in_ref[...].reshape(own_ref.shape)


def own_rows(hidden):
    reqs, steps, width = hidden.shape
    return pl.pallas_call(
        own_kernel,
        out_shape=jax.ShapeDtypeStruct((reqs * steps, width), BF16),
        in_specs=[VMEM],
        out_specs=VMEM,
        compiler_params=pltpu.CompilerParams(vmem_limit_bytes=2 * 1024 * 1024),
    )(hidden)


def collect_kernel(own_ref, *refs):
    *blocks, out_ref = refs
    rows, width = own_ref.shape
    out_ref[pl.ds(0, rows), :] = own_ref[...]
    for i, block in enumerate(blocks):
        out_ref[pl.ds(rows * (i + 1), rows), :] = block[...].reshape(rows, width)


def collect(own, blocks):
    rows, width = own.shape
    return pl.pallas_call(
        collect_kernel,
        out_shape=jax.ShapeDtypeStruct(((1 + len(blocks)) * rows, width), BF16),
        in_specs=[VMEM] * (1 + len(blocks)),
        out_specs=VMEM,
        compiler_params=pltpu.CompilerParams(vmem_limit_bytes=4 * 1024 * 1024),
        cost_estimate=pl.CostEstimate(
            flops=40_000_000_000, bytes_accessed=40_000_000, transcendentals=0
        ),
    )(own, *blocks)


NEAR = (2, 1, 3)
FAR = (3, 1, 2)


def shifted(array, first, amount, grid_rows, grid_cols):
    side = math.isqrt(grid_cols)
    pairs = []
    for row in range(grid_rows):
        for col in range(grid_cols):
            high, low = col // side, col % side
            if (row % 2 == 0) == first:
                low = (low + amount) % side
            else:
                high = (high + amount) % side
            pairs.append((row * grid_cols + col, row * grid_cols + high * side + low))
    return lax.ppermute(array, ("erow", "ecol"), pairs)


def place_of(piece, block, side):
    row, col = lax.axis_index("erow"), lax.axis_index("ecol")
    later, earlier = (0, *FAR)[piece], (0, *NEAR)[block]
    even = lax.rem(row, 2) == 0
    high = lax.div(col, side) + side - jnp.where(even, later, earlier)
    low = lax.rem(col, side) + side - jnp.where(even, earlier, later)
    return lax.rem(high, side) * side + lax.rem(low, side)


def attend_kernel(steps, index, side, *refs):
    (
        tok_ref,
        wq_ref,
        wk_ref,
        wv_ref,
        wb_ref,
        dl_ref,
        db_ref,
        ng_ref,
        dd_ref,
        gd_ref,
        du_ref,
        gl_ref,
        wo_ref,
        mem_ref,
    ) = refs[:14]
    (
        part_ref,
        keys_ref,
        upd_ref,
        stage,
        probe,
        reply,
    ) = refs[14:]
    width, hk = wq_ref.shape
    rows = stage.shape[1]
    reqs = rows // steps
    per_block = reqs // side
    places = [place_of(index, i, side) for i in range(side)]
    tok = tok_ref[...]

    def project(weight):
        return jnp.dot(tok, weight, preferred_element_type=F32)

    query = project(wq_ref[...])
    key = project(wk_ref[...])
    value = project(wv_ref[...])
    beta = jnp.sum(tok.astype(F32) * wb_ref[...].astype(F32), -1, keepdims=True)
    low_decay = project(dd_ref[...]).astype(BF16)
    low_gate = project(gd_ref[...]).astype(BF16)
    decay_pre = jnp.dot(low_decay, du_ref[...], preferred_element_type=F32)
    decay_pre = decay_pre + db_ref[...]
    gate = jax.nn.sigmoid(jnp.dot(low_gate, gl_ref[...], preferred_element_type=F32))
    softplus = jnp.maximum(decay_pre, 0.0) + jnp.log1p(jnp.exp(-jnp.abs(decay_pre)))
    stage[0] = unit_rows(query) * hk ** (-0.5)
    stage[1] = unit_rows(key)
    stage[2] = value
    stage[3] = jnp.broadcast_to(jax.nn.sigmoid(beta), (rows, hk))
    rate = jnp.exp(jnp.full((1, hk), dl_ref[0], F32))
    stage[4] = jnp.exp(-rate * softplus)

    def at(kind, t):
        return stage[kind, pl.ds(t, reqs, stride=steps), :]

    q = [at(0, t) for t in range(steps)]
    k = [at(1, t) for t in range(steps)]
    f = [at(4, t) for t in range(steps)]
    start = []
    for t in range(steps):
        start.append(f[0] if t == 0 else start[-1] * f[t])
        probe[pl.ds(t, reqs, stride=2 * steps), :] = start[t] * k[t]
        probe[pl.ds(steps + t, reqs, stride=2 * steps), :] = start[t] * q[t]

    for r in range(reqs):
        at_rows = pl.ds(r * 2 * steps, 2 * steps)
        memory = mem_ref[places[r // per_block] * per_block + r % per_block]
        reply[at_rows, :] = jnp.dot(
            probe[at_rows, :].astype(BF16), memory.astype(BF16), preferred_element_type=F32
        )

    decayed = []
    updates = []
    for t in range(steps):
        if t > 0:
            decayed = [row * f[t] for row in decayed]
        predicted = reply[pl.ds(t, reqs, stride=2 * steps), :]
        for s in range(t):
            predicted = predicted + jnp.sum(decayed[s] * k[t], -1, keepdims=True) * updates[s]
        updates.append(at(3, t) * (at(2, t) - predicted))
        decayed.append(k[t])
        head = reply[pl.ds(steps + t, reqs, stride=2 * steps), :]
        for s in range(t + 1):
            head = head + jnp.sum(decayed[s] * q[t], -1, keepdims=True) * updates[s]
        stage[0, pl.ds(t, reqs, stride=steps), :] = head
    for t in range(steps):
        keys_ref[pl.ds(t, reqs, stride=2 * steps), :] = decayed[t]
        keys_ref[pl.ds(steps + t, reqs, stride=2 * steps), :] = start[-1]
        upd_ref[pl.ds(t, reqs, stride=2 * steps), :] = updates[t]
        upd_ref[pl.ds(steps + t, reqs, stride=2 * steps), :] = jnp.zeros_like(updates[t])
    mixed = (rms_scale(stage[0]) * ng_ref[...] * gate).astype(BF16)
    part_ref[...] = jnp.dot(mixed, wo_ref[...], preferred_element_type=F32).astype(BF16)


def attend(index, side, piece, operands, steps):
    rows, width = piece.shape
    hk = operands[-1].shape[-1]
    in_specs = [VMEM] * (1 + len(operands))
    in_specs[5] = pl.BlockSpec(memory_space=pltpu.SMEM)
    return pl.pallas_call(
        functools.partial(attend_kernel, steps, index, side),
        out_shape=(
            jax.ShapeDtypeStruct((rows, width), BF16),
            jax.ShapeDtypeStruct((2 * rows, hk), F32),
            jax.ShapeDtypeStruct((2 * rows, hk), F32),
        ),
        in_specs=in_specs,
        out_specs=(VMEM,) * 3,
        scratch_shapes=[
            pltpu.VMEM((5, rows, hk), F32),
            pltpu.VMEM((2 * rows, hk), F32),
            pltpu.VMEM((2 * rows, hk), F32),
        ],
        compiler_params=pltpu.CompilerParams(vmem_limit_bytes=8 * 1024 * 1024),
        cost_estimate=pl.CostEstimate(
            flops=1_500_000_000, bytes_accessed=2_000_000, transcendentals=0
        ),
    )(piece, *operands)


def middle_kernel(here_ref, *refs):
    count = (len(refs) - 1) // 2
    total = here_ref[...].astype(F32)
    for ref in refs[:count]:
        total = total + ref[...].astype(F32)
    rows = refs[count].shape[0]
    refs[count][...] = total[:rows]
    for i, ref in enumerate(refs[count + 1 :]):
        ref[...] = total[rows * (i + 1) : rows * (i + 2)].astype(BF16)


def middle(here, terms):
    width = here.shape[1]
    rows = here.shape[0] // (1 + len(terms))
    return pl.pallas_call(
        middle_kernel,
        out_shape=(jax.ShapeDtypeStruct((rows, width), F32),)
        + (jax.ShapeDtypeStruct((rows, width), BF16),) * len(terms),
        in_specs=[VMEM] * (1 + len(terms)),
        out_specs=(VMEM,) * (1 + len(terms)),
        compiler_params=pltpu.CompilerParams(vmem_limit_bytes=4 * 1024 * 1024),
    )(here, *terms)


def state_kernel(steps, side, *refs):
    keys, upds = refs[:side], refs[side : 2 * side]
    mem_ref, new_hbm, new, store_sem = refs[2 * side :]
    size, hk = mem_ref.shape[0] // side**2, mem_ref.shape[-1]
    shape = (2 * steps * size, hk * size)
    own = lax.broadcasted_iota(jnp.int32, shape, 0) // (2 * steps) == (
        lax.broadcasted_iota(jnp.int32, shape, 1) // hk
    )
    stores = []
    for b in range(side**2):
        piece, block = b // side, b % side
        height = 2 * steps
        rows = pl.ds(height * size * block, height * size)
        columns = keys[piece][rows, :].T
        change = jnp.dot(
            columns.astype(BF16),
            jnp.where(own, jnp.concatenate([upds[piece][rows, :]] * size, 1), 0.0).astype(BF16),
            preferred_element_type=F32,
        )
        start = place_of(piece, block, side) * size
        for r in range(size):
            decay = columns[:, height * r + steps : height * r + steps + 1]
            new[b, r] = mem_ref[start + r] * decay + change[:, hk * r : hk * (r + 1)]
        stores.append(
            pltpu.make_async_copy(new.at[b], new_hbm.at[pl.ds(start, size)], store_sem.at[b])
        )
        stores[-1].start()
    for store in stores:
        store.wait()


def new_memory(keys, updates, memory, steps):
    reqs, hk, _ = memory.shape
    side = len(keys)
    return pl.pallas_call(
        functools.partial(state_kernel, steps, side),
        out_shape=pltpu.HBM(memory.shape, F32),
        in_specs=[VMEM] * (2 * side + 1),
        out_specs=HBM,
        scratch_shapes=[
            pltpu.VMEM((side**2, reqs // side**2, hk, hk), F32),
            pltpu.SemaphoreType.DMA((side**2,)),
        ],
        compiler_params=pltpu.CompilerParams(vmem_limit_bytes=16 * 1024 * 1024),
        cost_estimate=pl.CostEstimate(
            flops=9 * reqs * hk * hk, bytes_accessed=2 * reqs * hk * hk * 4, transcendentals=0
        ),
    )(*keys, *updates, memory)


def route_kernel(capacity, ids_ref, weights_ref, place_ref, combine_ref):
    rows, slots = combine_ref.shape
    picks = ids_ref.shape[-1]
    ids = ids_ref[...].reshape(rows, picks)
    weights = weights_ref[...].reshape(rows, picks)
    slot = lax.broadcasted_iota(jnp.int32, (rows, slots), 1)
    named = jnp.zeros((rows, slots), F32)
    weight = jnp.zeros((rows, slots), F32)
    for j in range(picks):
        hit = ids[:, j : j + 1] == slot // capacity
        named = jnp.where(hit, 1.0, named)
        weight = jnp.where(hit, weights[:, j : j + 1], weight)
    row = lax.broadcasted_iota(jnp.int32, (rows, rows), 0)
    earlier = (lax.broadcasted_iota(jnp.int32, (rows, rows), 1) < row).astype(BF16)
    number = jnp.dot(earlier, named.astype(BF16), preferred_element_type=F32)
    mine = (named > 0.0) & (number == (slot % capacity).astype(F32))
    place_ref[...] = jnp.where(mine, 1.0, 0.0).astype(BF16)
    combine_ref[...] = jnp.where(mine, weight, 0.0)


def route(ids, weights, capacity, slots):
    rows = ids.shape[0] * ids.shape[1]
    return pl.pallas_call(
        functools.partial(route_kernel, capacity),
        out_shape=(
            jax.ShapeDtypeStruct((rows, slots), BF16),
            jax.ShapeDtypeStruct((rows, slots), F32),
        ),
        in_specs=[VMEM] * 2,
        out_specs=(VMEM,) * 2,
        compiler_params=pltpu.CompilerParams(vmem_limit_bytes=2 * 1024 * 1024),
    )(ids, weights)


def join_kernel(own_ref, gain_ref, place_ref, *refs):
    *terms, residual_ref, out_ref = refs
    attended = terms[0][...]
    for ref in terms[1:]:
        attended = attended + ref[...].astype(F32)
    residual = (own_ref[...].astype(F32) + attended).astype(BF16)
    residual_ref[...] = residual
    gain = gain_ref[...].reshape(1, -1)
    normed = (rms_scale(residual.astype(F32)) * gain).astype(BF16)
    sent = lax.dot_general(
        place_ref[...], normed, (((0,), (0,)), ((), ())), preferred_element_type=F32
    ).astype(BF16)
    out_ref[...] = sent.reshape(out_ref.shape)


def join(terms, own, gain, placing, shape):
    rows, width = own.shape
    return pl.pallas_call(
        join_kernel,
        out_shape=(
            jax.ShapeDtypeStruct((rows, width), BF16),
            jax.ShapeDtypeStruct(shape, BF16),
        ),
        in_specs=[VMEM] * (3 + len(terms)),
        out_specs=(VMEM, VMEM),
        compiler_params=pltpu.CompilerParams(vmem_limit_bytes=8 * 1024 * 1024),
        cost_estimate=pl.CostEstimate(
            flops=40_000_000_000, bytes_accessed=40_000_000, transcendentals=0
        ),
    )(own, gain, placing, *terms)


def expert_kernel(rows_ref, gate_ref, up_ref, down_ref, out_ref):
    rows = rows_ref[...].reshape(-1, rows_ref.shape[-1])
    gate = jnp.dot(rows, gate_ref[...], preferred_element_type=F32)
    up = jnp.dot(rows, up_ref[...], preferred_element_type=F32)
    hidden = (jax.nn.silu(gate) * up).astype(BF16)
    out = jnp.dot(hidden, down_ref[...], preferred_element_type=F32).astype(BF16)
    out_ref[...] = out.reshape(out_ref.shape)


def run_expert(rows, gate, up, down):
    width, hidden = gate.shape
    count = rows.size // width
    return pl.pallas_call(
        expert_kernel,
        out_shape=jax.ShapeDtypeStruct(rows.shape, BF16),
        in_specs=[VMEM] * 4,
        out_specs=VMEM,
        compiler_params=pltpu.CompilerParams(vmem_limit_bytes=24 * 1024 * 1024),
        cost_estimate=pl.CostEstimate(
            flops=6 * count * width * hidden,
            bytes_accessed=6 * width * hidden + 4 * count * width,
            transcendentals=count * hidden,
        ),
    )(rows, gate, up, down)


def combine_kernel(rows_ref, residual_ref, weight_ref, out_ref):
    rows = rows_ref[...].reshape(-1, rows_ref.shape[-1])
    weight = weight_ref[...]
    high = weight.astype(BF16)
    rest = weight - high.astype(F32)
    middle = rest.astype(BF16)
    low = (rest - middle.astype(F32)).astype(BF16)
    count = weight.shape[0]
    three = jnp.dot(jnp.concatenate([high, middle, low], 0), rows, preferred_element_type=F32)
    routed = three[:count] + (three[count : 2 * count] + three[2 * count :])
    mixed = (residual_ref[...].astype(F32) + routed).astype(BF16)
    out_ref[...] = mixed.reshape(out_ref.shape)


def combine_rows(rows, residual, weight, shape):
    return pl.pallas_call(
        combine_kernel,
        out_shape=jax.ShapeDtypeStruct(shape, BF16),
        in_specs=[VMEM] * 3,
        out_specs=VMEM,
        compiler_params=pltpu.CompilerParams(vmem_limit_bytes=8 * 1024 * 1024),
    )(rows, residual, weight)


def local(
    hidden_in,
    kda_state,
    query_weight,
    key_weight,
    value_weight,
    beta_weight,
    decay_down,
    decay_up,
    decay_log,
    decay_bias,
    gate_down,
    gate_lift,
    norm_gain,
    output_weight,
    ffn_gain,
    expert_ids,
    route_weight,
    expert_gate,
    expert_up,
    expert_down,
):
    local_req, step_count, model_width = hidden_in.shape
    head_size = kda_state.shape[-1]
    grid_rows = lax.axis_size("erow")
    grid_cols = lax.axis_size("ecol")
    side = math.isqrt(grid_cols)
    own = own_rows(hidden_in)

    def move(array, first, amount):
        return shifted(array, first, amount, grid_rows, grid_cols)

    near = collect(own, [move(hidden_in, True, amount) for amount in NEAR])
    pieces = [near] + [move(near, False, amount) for amount in FAR]
    memory = kda_state.reshape(kda_state.shape[0], head_size, head_size)
    operands = (
        query_weight,
        key_weight,
        value_weight,
        beta_weight.reshape(1, model_width),
        decay_log,
        decay_bias.reshape(1, head_size),
        norm_gain.reshape(1, head_size),
        decay_down,
        gate_down,
        decay_up,
        gate_lift,
        output_weight,
        memory,
    )
    done = [attend(index, side, piece, operands, step_count) for index, piece in enumerate(pieces)]
    parts, keys, updates = zip(*done)
    returned = [move(part, False, -amount) for part, amount in zip(parts[1:], FAR)]
    new_state = new_memory(keys, updates, memory, step_count)
    new_state, first = lax.optimization_barrier((new_state, parts[0]))
    here, *others = middle(first, returned)
    terms = [here] + [move(other, True, -amount) for other, amount in zip(others, NEAR)]
    device_count = grid_rows * grid_cols
    row_total, pick_count = local_req * step_count, expert_ids.shape[-1]
    capacity = max(2, 2 * row_total * pick_count // device_count)
    slots_total = device_count * capacity
    placing, combine = route(expert_ids, route_weight, capacity, slots_total)
    residual, outgoing = join(
        terms, own, ffn_gain, placing, (device_count, capacity, model_width)
    )
    received = lax.all_to_all(
        outgoing, ("erow", "ecol"), split_axis=0, concat_axis=0, tiled=True
    )
    produced = run_expert(received, expert_gate[0], expert_up[0], expert_down[0])
    returned = lax.all_to_all(
        produced, ("erow", "ecol"), split_axis=0, concat_axis=0, tiled=True
    )
    mixed = combine_rows(returned, residual, combine, hidden_in.shape)
    return (mixed, new_state.reshape(kda_state.shape))


def solution(mesh):
    return jax.shard_map(
        local,
        mesh=mesh,
        in_specs=(
            P(("erow", "ecol"), None, None),
            P("erow", "ecol", None, None),
            P(None, "ecol"),
            P(None, "ecol"),
            P(None, "ecol"),
            P(None, "ecol"),
            P(),
            P(None, "ecol"),
            P("ecol"),
            P("ecol"),
            P(),
            P(None, "ecol"),
            P(),
            P("ecol", None),
            P(),
            P(("erow", "ecol"), None, None),
            P(("erow", "ecol"), None, None),
            P(("erow", "ecol"), None, None),
            P(("erow", "ecol"), None, None),
            P(("erow", "ecol"), None, None),
        ),
        out_specs=(P(("erow", "ecol"), None, None), P("erow", "ecol", None, None)),
        check_vma=False,
    )
```

```python
import functools
import math

import jax
import jax.numpy as jnp
from jax import lax
from jax.experimental import pallas as pl
from jax.experimental.pallas import tpu as pltpu
from jax.sharding import PartitionSpec as P

EPSILON = 1e-06
F32 = jnp.float32
BF16 = jnp.bfloat16
VMEM = pl.BlockSpec(memory_space=pltpu.VMEM)
HBM = pl.BlockSpec(memory_space=pltpu.HBM)


def in_hbm(array):
    return pltpu.with_memory_space_constraint(array, pltpu.HBM)


def unit_rows(vectors):
    return vectors * lax.rsqrt(jnp.sum(vectors * vectors, -1, keepdims=True) + EPSILON)


def rms_scale(vectors):
    return vectors * lax.rsqrt(jnp.mean(vectors * vectors, -1, keepdims=True) + EPSILON)


def own_kernel(in_ref, own_ref):
    own_ref[...] = in_ref[...].reshape(own_ref.shape)


def own_rows(hidden):
    reqs, steps, width = hidden.shape
    return pl.pallas_call(
        own_kernel,
        out_shape=jax.ShapeDtypeStruct((reqs * steps, width), BF16),
        in_specs=[VMEM],
        out_specs=VMEM,
        compiler_params=pltpu.CompilerParams(vmem_limit_bytes=2 * 1024 * 1024),
    )(hidden)


def collect_kernel(own_ref, *refs):
    *blocks, out_ref = refs
    rows, width = own_ref.shape
    out_ref[pl.ds(0, rows), :] = own_ref[...]
    for i, block in enumerate(blocks):
        out_ref[pl.ds(rows * (i + 1), rows), :] = block[...].reshape(rows, width)


def collect(own, blocks):
    rows, width = own.shape
    return pl.pallas_call(
        collect_kernel,
        out_shape=jax.ShapeDtypeStruct(((1 + len(blocks)) * rows, width), BF16),
        in_specs=[VMEM] * (1 + len(blocks)),
        out_specs=VMEM,
        compiler_params=pltpu.CompilerParams(vmem_limit_bytes=4 * 1024 * 1024),
        cost_estimate=pl.CostEstimate(
            flops=40_000_000_000, bytes_accessed=40_000_000, transcendentals=0
        ),
    )(own, *blocks)


NEAR = (1, 2, 3)
FAR = (3, 1, 2)


def shifted(array, first, amount, grid_rows, grid_cols):
    side = math.isqrt(grid_cols)
    pairs = []
    for row in range(grid_rows):
        for col in range(grid_cols):
            high, low = col // side, col % side
            if (row % 2 == 0) == first:
                low = (low + amount) % side
            else:
                high = (high + amount) % side
            pairs.append((row * grid_cols + col, row * grid_cols + high * side + low))
    return lax.ppermute(array, ("erow", "ecol"), pairs)


def place_of(piece, block, side):
    row, col = lax.axis_index("erow"), lax.axis_index("ecol")
    later, earlier = (0, *FAR)[piece], (0, *NEAR)[block]
    even = lax.rem(row, 2) == 0
    high = lax.div(col, side) + side - jnp.where(even, later, earlier)
    low = lax.rem(col, side) + side - jnp.where(even, earlier, later)
    return lax.rem(high, side) * side + lax.rem(low, side)


def attend_kernel(steps, index, side, *refs):
    (
        tok_ref,
        wq_ref,
        wk_ref,
        wv_ref,
        wb_ref,
        dl_ref,
        db_ref,
        ng_ref,
        dd_ref,
        gd_ref,
        du_ref,
        gl_ref,
        wo_ref,
        mem_ref,
    ) = refs[:14]
    (
        part_ref,
        keys_ref,
        upd_ref,
        stage,
        probe,
        reply,
    ) = refs[14:]
    width, hk = wq_ref.shape
    rows = stage.shape[1]
    reqs = rows // steps
    per_block = reqs // side
    places = [place_of(index, i, side) for i in range(side)]
    tok = tok_ref[...]

    def project(weight):
        return jnp.dot(tok, weight, preferred_element_type=F32)

    query = project(wq_ref[...])
    key = project(wk_ref[...])
    value = project(wv_ref[...])
    beta = jnp.sum(tok.astype(F32) * wb_ref[...].astype(F32), -1, keepdims=True)
    low_decay = project(dd_ref[...]).astype(BF16)
    low_gate = project(gd_ref[...]).astype(BF16)
    decay_pre = jnp.dot(low_decay, du_ref[...], preferred_element_type=F32)
    decay_pre = decay_pre + db_ref[...]
    gate = jax.nn.sigmoid(jnp.dot(low_gate, gl_ref[...], preferred_element_type=F32))
    softplus = jnp.maximum(decay_pre, 0.0) + jnp.log1p(jnp.exp(-jnp.abs(decay_pre)))
    stage[0] = unit_rows(query) * hk ** (-0.5)
    stage[1] = unit_rows(key)
    stage[2] = value
    stage[3] = jnp.broadcast_to(jax.nn.sigmoid(beta), (rows, hk))
    rate = jnp.exp(jnp.full((1, hk), dl_ref[0], F32))
    stage[4] = jnp.exp(-rate * softplus)

    def at(kind, t):
        return stage[kind, pl.ds(t, reqs, stride=steps), :]

    q = [at(0, t) for t in range(steps)]
    k = [at(1, t) for t in range(steps)]
    f = [at(4, t) for t in range(steps)]
    start = []
    for t in range(steps):
        start.append(f[0] if t == 0 else start[-1] * f[t])
        probe[pl.ds(t, reqs, stride=2 * steps), :] = start[t] * k[t]
        probe[pl.ds(steps + t, reqs, stride=2 * steps), :] = start[t] * q[t]

    for r in range(reqs):
        at_rows = pl.ds(r * 2 * steps, 2 * steps)
        memory = mem_ref[places[r // per_block] * per_block + r % per_block]
        reply[at_rows, :] = jnp.dot(
            probe[at_rows, :].astype(BF16), memory.astype(BF16), preferred_element_type=F32
        )

    decayed = []
    updates = []
    for t in range(steps):
        if t > 0:
            decayed = [row * f[t] for row in decayed]
        predicted = reply[pl.ds(t, reqs, stride=2 * steps), :]
        for s in range(t):
            predicted = predicted + jnp.sum(decayed[s] * k[t], -1, keepdims=True) * updates[s]
        updates.append(at(3, t) * (at(2, t) - predicted))
        decayed.append(k[t])
        head = reply[pl.ds(steps + t, reqs, stride=2 * steps), :]
        for s in range(t + 1):
            head = head + jnp.sum(decayed[s] * q[t], -1, keepdims=True) * updates[s]
        stage[0, pl.ds(t, reqs, stride=steps), :] = head
    for t in range(steps):
        keys_ref[pl.ds(t, reqs, stride=2 * steps), :] = decayed[t]
        keys_ref[pl.ds(steps + t, reqs, stride=2 * steps), :] = start[-1]
        upd_ref[pl.ds(t, reqs, stride=2 * steps), :] = updates[t]
        upd_ref[pl.ds(steps + t, reqs, stride=2 * steps), :] = jnp.zeros_like(updates[t])
    mixed = (rms_scale(stage[0]) * ng_ref[...] * gate).astype(BF16)
    part_ref[...] = jnp.dot(mixed, wo_ref[...], preferred_element_type=F32).astype(BF16)


def attend(index, side, piece, operands, steps):
    rows, width = piece.shape
    hk = operands[-1].shape[-1]
    in_specs = [VMEM] * (1 + len(operands))
    in_specs[5] = pl.BlockSpec(memory_space=pltpu.SMEM)
    return pl.pallas_call(
        functools.partial(attend_kernel, steps, index, side),
        out_shape=(
            jax.ShapeDtypeStruct((rows, width), BF16),
            jax.ShapeDtypeStruct((2 * rows, hk), F32),
            jax.ShapeDtypeStruct((2 * rows, hk), F32),
        ),
        in_specs=in_specs,
        out_specs=(VMEM,) * 3,
        scratch_shapes=[
            pltpu.VMEM((5, rows, hk), F32),
            pltpu.VMEM((2 * rows, hk), F32),
            pltpu.VMEM((2 * rows, hk), F32),
        ],
        compiler_params=pltpu.CompilerParams(vmem_limit_bytes=8 * 1024 * 1024),
        cost_estimate=pl.CostEstimate(
            flops=1_500_000_000, bytes_accessed=2_000_000, transcendentals=0
        ),
    )(piece, *operands)


def middle_kernel(here_ref, *refs):
    count = (len(refs) - 1) // 2
    total = here_ref[...].astype(F32)
    for ref in refs[:count]:
        total = total + ref[...].astype(F32)
    rows = refs[count].shape[0]
    refs[count][...] = total[:rows]
    for i, ref in enumerate(refs[count + 1 :]):
        ref[...] = total[rows * (i + 1) : rows * (i + 2)].astype(BF16)


def middle(here, terms):
    width = here.shape[1]
    rows = here.shape[0] // (1 + len(terms))
    return pl.pallas_call(
        middle_kernel,
        out_shape=(jax.ShapeDtypeStruct((rows, width), F32),)
        + (jax.ShapeDtypeStruct((rows, width), BF16),) * len(terms),
        in_specs=[VMEM] * (1 + len(terms)),
        out_specs=(VMEM,) * (1 + len(terms)),
        compiler_params=pltpu.CompilerParams(vmem_limit_bytes=4 * 1024 * 1024),
    )(here, *terms)


def state_kernel(steps, side, *refs):
    keys, upds = refs[:side], refs[side : 2 * side]
    mem_ref, new_hbm, new, store_sem = refs[2 * side :]
    size, hk = mem_ref.shape[0] // side**2, mem_ref.shape[-1]
    shape = (2 * steps * size, hk * size)
    own = lax.broadcasted_iota(jnp.int32, shape, 0) // (2 * steps) == (
        lax.broadcasted_iota(jnp.int32, shape, 1) // hk
    )
    stores = []
    for b in range(side**2):
        piece, block = b // side, b % side
        height = 2 * steps
        rows = pl.ds(height * size * block, height * size)
        columns = keys[piece][rows, :].T
        change = jnp.dot(
            columns.astype(BF16),
            jnp.where(own, jnp.concatenate([upds[piece][rows, :]] * size, 1), 0.0).astype(BF16),
            preferred_element_type=F32,
        )
        start = place_of(piece, block, side) * size
        for r in range(size):
            decay = columns[:, height * r + steps : height * r + steps + 1]
            new[b, r] = mem_ref[start + r] * decay + change[:, hk * r : hk * (r + 1)]
        stores.append(
            pltpu.make_async_copy(new.at[b], new_hbm.at[pl.ds(start, size)], store_sem.at[b])
        )
        stores[-1].start()
    for store in stores:
        store.wait()


def new_memory(keys, updates, memory, steps):
    reqs, hk, _ = memory.shape
    side = len(keys)
    return pl.pallas_call(
        functools.partial(state_kernel, steps, side),
        out_shape=pltpu.HBM(memory.shape, F32),
        in_specs=[VMEM] * (2 * side + 1),
        out_specs=HBM,
        scratch_shapes=[
            pltpu.VMEM((side**2, reqs // side**2, hk, hk), F32),
            pltpu.SemaphoreType.DMA((side**2,)),
        ],
        compiler_params=pltpu.CompilerParams(vmem_limit_bytes=16 * 1024 * 1024),
        cost_estimate=pl.CostEstimate(
            flops=9 * reqs * hk * hk, bytes_accessed=2 * reqs * hk * hk * 4, transcendentals=0
        ),
    )(*keys, *updates, memory)


def route_kernel(capacity, ids_ref, weights_ref, place_ref, combine_ref):
    rows, slots = combine_ref.shape
    picks = ids_ref.shape[-1]
    ids = ids_ref[...].reshape(rows, picks)
    weights = weights_ref[...].reshape(rows, picks)
    slot = lax.broadcasted_iota(jnp.int32, (rows, slots), 1)
    named = jnp.zeros((rows, slots), F32)
    weight = jnp.zeros((rows, slots), F32)
    for j in range(picks):
        hit = ids[:, j : j + 1] == slot // capacity
        named = jnp.where(hit, 1.0, named)
        weight = jnp.where(hit, weights[:, j : j + 1], weight)
    row = lax.broadcasted_iota(jnp.int32, (rows, rows), 0)
    earlier = (lax.broadcasted_iota(jnp.int32, (rows, rows), 1) < row).astype(BF16)
    number = jnp.dot(earlier, named.astype(BF16), preferred_element_type=F32)
    mine = (named > 0.0) & (number == (slot % capacity).astype(F32))
    place_ref[...] = jnp.where(mine, 1.0, 0.0).astype(BF16)
    combine_ref[...] = jnp.where(mine, weight, 0.0)


def route(ids, weights, capacity, slots):
    rows = ids.shape[0] * ids.shape[1]
    return pl.pallas_call(
        functools.partial(route_kernel, capacity),
        out_shape=(
            jax.ShapeDtypeStruct((rows, slots), BF16),
            jax.ShapeDtypeStruct((rows, slots), F32),
        ),
        in_specs=[VMEM] * 2,
        out_specs=(VMEM,) * 2,
        compiler_params=pltpu.CompilerParams(vmem_limit_bytes=2 * 1024 * 1024),
    )(ids, weights)


def join_kernel(own_ref, gain_ref, place_ref, *refs):
    *terms, residual_ref, out_ref = refs
    attended = terms[0][...]
    for ref in terms[1:]:
        attended = attended + ref[...].astype(F32)
    residual = (own_ref[...].astype(F32) + attended).astype(BF16)
    residual_ref[...] = residual
    gain = gain_ref[...].reshape(1, -1)
    normed = (rms_scale(residual.astype(F32)) * gain).astype(BF16)
    sent = lax.dot_general(
        place_ref[...], normed, (((0,), (0,)), ((), ())), preferred_element_type=F32
    ).astype(BF16)
    out_ref[...] = sent.reshape(out_ref.shape)


def join(terms, own, gain, placing, shape):
    rows, width = own.shape
    return pl.pallas_call(
        join_kernel,
        out_shape=(
            jax.ShapeDtypeStruct((rows, width), BF16),
            jax.ShapeDtypeStruct(shape, BF16),
        ),
        in_specs=[VMEM] * (3 + len(terms)),
        out_specs=(VMEM, VMEM),
        compiler_params=pltpu.CompilerParams(vmem_limit_bytes=8 * 1024 * 1024),
        cost_estimate=pl.CostEstimate(
            flops=40_000_000_000, bytes_accessed=40_000_000, transcendentals=0
        ),
    )(own, gain, placing, *terms)


def expert_kernel(rows_ref, gate_ref, up_ref, down_ref, out_ref):
    rows = rows_ref[...].reshape(-1, rows_ref.shape[-1])
    gate = jnp.dot(rows, gate_ref[...], preferred_element_type=F32)
    up = jnp.dot(rows, up_ref[...], preferred_element_type=F32)
    hidden = (jax.nn.silu(gate) * up).astype(BF16)
    out = jnp.dot(hidden, down_ref[...], preferred_element_type=F32).astype(BF16)
    out_ref[...] = out.reshape(out_ref.shape)


def run_expert(rows, gate, up, down):
    width, hidden = gate.shape
    count = rows.size // width
    return pl.pallas_call(
        expert_kernel,
        out_shape=jax.ShapeDtypeStruct(rows.shape, BF16),
        in_specs=[VMEM] * 4,
        out_specs=VMEM,
        compiler_params=pltpu.CompilerParams(vmem_limit_bytes=24 * 1024 * 1024),
        cost_estimate=pl.CostEstimate(
            flops=6 * count * width * hidden,
            bytes_accessed=6 * width * hidden + 4 * count * width,
            transcendentals=count * hidden,
        ),
    )(rows, gate, up, down)


def combine_kernel(rows_ref, residual_ref, weight_ref, out_ref):
    rows = rows_ref[...].reshape(-1, rows_ref.shape[-1])
    weight = weight_ref[...]
    high = weight.astype(BF16)
    rest = weight - high.astype(F32)
    middle = rest.astype(BF16)
    low = (rest - middle.astype(F32)).astype(BF16)
    count = weight.shape[0]
    three = jnp.dot(jnp.concatenate([high, middle, low], 0), rows, preferred_element_type=F32)
    routed = three[:count] + (three[count : 2 * count] + three[2 * count :])
    mixed = (residual_ref[...].astype(F32) + routed).astype(BF16)
    out_ref[...] = mixed.reshape(out_ref.shape)


def combine_rows(rows, residual, weight, shape):
    return pl.pallas_call(
        combine_kernel,
        out_shape=jax.ShapeDtypeStruct(shape, BF16),
        in_specs=[VMEM] * 3,
        out_specs=VMEM,
        compiler_params=pltpu.CompilerParams(vmem_limit_bytes=8 * 1024 * 1024),
    )(rows, residual, weight)


def local(
    hidden_in,
    kda_state,
    query_weight,
    key_weight,
    value_weight,
    beta_weight,
    decay_down,
    decay_up,
    decay_log,
    decay_bias,
    gate_down,
    gate_lift,
    norm_gain,
    output_weight,
    ffn_gain,
    expert_ids,
    route_weight,
    expert_gate,
    expert_up,
    expert_down,
):
    local_req, step_count, model_width = hidden_in.shape
    head_size = kda_state.shape[-1]
    grid_rows = lax.axis_size("erow")
    grid_cols = lax.axis_size("ecol")
    side = math.isqrt(grid_cols)
    own = own_rows(hidden_in)

    def move(array, first, amount):
        return shifted(array, first, amount, grid_rows, grid_cols)

    near = collect(own, [move(hidden_in, True, amount) for amount in NEAR])
    pieces = [near] + [move(near, False, amount) for amount in FAR]
    memory = kda_state.reshape(kda_state.shape[0], head_size, head_size)
    operands = (
        query_weight,
        key_weight,
        value_weight,
        beta_weight.reshape(1, model_width),
        decay_log,
        decay_bias.reshape(1, head_size),
        norm_gain.reshape(1, head_size),
        decay_down,
        gate_down,
        decay_up,
        gate_lift,
        output_weight,
        memory,
    )
    done = [attend(index, side, piece, operands, step_count) for index, piece in enumerate(pieces)]
    parts, keys, updates = zip(*done)
    returned = [move(part, False, -amount) for part, amount in zip(parts[1:], FAR)]
    new_state = new_memory(keys, updates, memory, step_count)
    new_state, first = lax.optimization_barrier((new_state, parts[0]))
    here, *others = middle(first, returned)
    terms = [here] + [move(other, True, -amount) for other, amount in zip(others, NEAR)]
    device_count = grid_rows * grid_cols
    row_total, pick_count = local_req * step_count, expert_ids.shape[-1]
    capacity = max(2, 2 * row_total * pick_count // device_count)
    slots_total = device_count * capacity
    placing, combine = route(expert_ids, route_weight, capacity, slots_total)
    residual, outgoing = join(
        terms, own, ffn_gain, placing, (device_count, capacity, model_width)
    )
    received = lax.all_to_all(
        outgoing, ("erow", "ecol"), split_axis=0, concat_axis=0, tiled=True
    )
    produced = run_expert(received, expert_gate[0], expert_up[0], expert_down[0])
    returned = lax.all_to_all(
        produced, ("erow", "ecol"), split_axis=0, concat_axis=0, tiled=True
    )
    mixed = combine_rows(returned, residual, combine, hidden_in.shape)
    return (mixed, new_state.reshape(kda_state.shape))


def solution(mesh):
    return jax.shard_map(
        local,
        mesh=mesh,
        in_specs=(
            P(("erow", "ecol"), None, None),
            P("erow", "ecol", None, None),
            P(None, "ecol"),
            P(None, "ecol"),
            P(None, "ecol"),
            P(None, "ecol"),
            P(),
            P(None, "ecol"),
            P("ecol"),
            P("ecol"),
            P(),
            P(None, "ecol"),
            P(),
            P("ecol", None),
            P(),
            P(("erow", "ecol"), None, None),
            P(("erow", "ecol"), None, None),
            P(("erow", "ecol"), None, None),
            P(("erow", "ecol"), None, None),
            P(("erow", "ecol"), None, None),
        ),
        out_specs=(P(("erow", "ecol"), None, None), P("erow", "ecol", None, None)),
        check_vma=False,
    )
```
